32 devices in a mesh: groups: 2 (over x), tm: 16 (over z, y, core).
Axes of the slice: x: 2, y: 2, z: 4, core: 2. Of those that a mesh axis runs over, the one named last changes fastest.
Arguments:
- frames: bfloat16 [8192, 1536], P(('groups', 'tm')), parts along dimension 0, may hold values from -6 to 6
- frame_count: int32 [32], P(('groups', 'tm')), parts along dimension 0, may hold values from 128 to 256, as said below
- lookback_mask: int32 [32, 4], P(('groups', 'tm')), parts along dimension 0, may hold values 0 or 1
- attn_gain: float32 [1536], replicated, may hold values from 0.1 to 1.9
- w_query: bfloat16 [1536, 768], P('tm')
- w_key: bfloat16 [1536, 768], P('tm')
- w_value: bfloat16 [1536, 768], P('tm'), may hold values from -0.15625 to 0.15625
- w_out: bfloat16 [768, 1536], P('tm'), may hold values from -0.21875 to 0.21875
- conv_gain: float32 [1536], replicated, may hold values from 0.1 to 1.9
- w_glu: bfloat16 [1536, 2048], P('tm'), may hold values from -0.15625 to 0.15625
- depthwise: float32 [31, 1024], replicated, may hold values from -1 to 1
- conv_scale: float32 [1024], replicated, may hold values from 0.5 to 2
- conv_shift: float32 [1024], replicated, may hold values from -3 to 3
- w_proj: bfloat16 [1024, 1536], P('tm'), may hold values from -0.1875 to 0.1875
Outputs:
- block_out: bfloat16 [8192, 1536], P(('groups', 'tm')), parts along dimension 0
The draws below stay inside these ranges and needn't reach their ends.
There are 2 independent parts, one for each index of `groups`. The reference program is written for one: setup_inputs(seed, part) draws one part's arguments, and reference() takes and returns one part's arrays. A program takes and returns all parts, laid end to end along the dimension named above; an argument that names none is the same for every part. Nothing has to cross between parts.
Inputs may be any that keep to these rules, and one draw needn't show every extreme that they name: `frame_count`: live frames of each span; the rest of its 256 frames are padding.
All inputs are finite; a program needn't handle non-finite values. No bound on the sum of `lookback_mask` on one device may be relied on, other than what follows from the above.
Results may differ from the reference program's by a relative error of at most 0.0095.
Values may be sent and summed in bfloat16 or wider, within the bound.
A program may use at most 128 MiB of HBM per device.

```python
import math
import jax
import jax.numpy as jnp
from jax import lax

D = 1536
HEADS = 8
HEAD_DIM = 96
CONV_CH = 1024
KERNEL = 31
FRAMES_DEV = 256
QKV = 768
SPANS = 16
FRAMES = 4096


def paired_weights(key):
    base_query = jax.random.normal(jax.random.fold_in(key, 11), (D, QKV), jnp.float32) * D ** (-0.5)
    base_key = jax.random.normal(jax.random.fold_in(key, 12), (D, QKV), jnp.float32) * D ** (-0.5)
    return (base_query, base_key)


def draw_w_query(key, part):
    return paired_weights(key)[0].astype(jnp.bfloat16)


def draw_w_key(key, part):
    return paired_weights(key)[1].astype(jnp.bfloat16)


def draw_frame_count(key, part):
    counts = jax.random.randint(jax.random.fold_in(key, 21), (SPANS,), FRAMES_DEV // 2, FRAMES_DEV + 1)
    fullest = jax.random.randint(jax.random.fold_in(key, 22), (), 0, SPANS)
    emptiest = (fullest + 1 + jax.random.randint(jax.random.fold_in(key, 23), (), 0, SPANS - 1)) % SPANS
    index = jnp.arange(SPANS)
    counts = jnp.where(index == fullest, FRAMES_DEV, jnp.where(index == emptiest, FRAMES_DEV // 2, counts))
    return counts.astype(jnp.int32)


def set_ends(values, key, least, largest):
    spot = [jax.random.randint(jax.random.fold_in(key, axis), (), 0, length) for axis, length in enumerate(values.shape)]
    longest = values.shape.index(max(values.shape))
    neighbour = spot[:longest] + [(spot[longest] + 1) % values.shape[longest]] + spot[longest + 1:]
    return values.at[tuple(spot)].set(least).at[tuple(neighbour)].set(largest)


def block_levels(stream_key, dims, pieces, least, largest):
    def one(dim, parts):
        heights = jax.random.uniform(jax.random.fold_in(jax.random.fold_in(stream_key, 6), dim), (parts,), jnp.float32, least / len(pieces), largest / len(pieces))
        return jnp.repeat(jnp.exp(heights), dims[dim] // parts).reshape((-1,) + (1,) * (len(dims) - dim - 1))

    level = one(*pieces[0])
    for cut in pieces[1:]:
        level = level * one(*cut)
    return level


def scatter_about(own_key, extent, scale, most, pieces=(), kind=jnp.bfloat16):
    entries = scale * jax.random.normal(own_key, extent, jnp.float32)
    if pieces:
        entries = entries * block_levels(own_key, extent, pieces, -0.22, 0.18)
    return jnp.clip(entries, -most, most).astype(kind)


def setup_inputs(seed: int = 0, part: int = 0) -> dict:
    key_list = jax.random.split(jax.random.key(seed), 15)
    part_keys = jax.random.split(jax.random.fold_in(key_list[14], part), 15)
    frames = scatter_about(part_keys[0], (FRAMES, D), 1.0, 6.0, ((0, 16),))
    frame_count = draw_frame_count(jax.random.fold_in(jax.random.fold_in(key_list[14], part), 71), part)
    lookback_mask = set_ends((jax.random.randint(part_keys[2], (SPANS, 4), 0, 4) < 3).astype(jnp.int32), jax.random.fold_in(part_keys[2], 1), 0, 1)
    attn_gain = jnp.clip(1.0 + 0.18 * jax.random.normal(key_list[3], (D,), jnp.float32), 0.1, 1.9)
    w_query = draw_w_query(jax.random.fold_in(key_list[14], 71), part)
    w_key = draw_w_key(jax.random.fold_in(key_list[14], 71), part)
    w_value = scatter_about(key_list[6], (D, QKV), D ** -0.5, 0.15625, ((0, 16),))
    w_out = scatter_about(key_list[7], (QKV, D), QKV ** -0.5, 0.21875, ((0, 16),))
    conv_gain = jnp.clip(1.0 + 0.18 * jax.random.normal(key_list[8], (D,), jnp.float32), 0.1, 1.9)
    w_glu = scatter_about(key_list[9], (D, 2 * CONV_CH), D ** -0.5, 0.15625, ((0, 16),))
    depthwise = scatter_about(key_list[10], (KERNEL, CONV_CH), KERNEL ** -0.5, 1.0, (), jnp.float32)
    conv_scale = jnp.clip(jnp.exp(jax.random.uniform(key_list[11], (CONV_CH,), jnp.float32, math.log(0.5), math.log(2.0))), 0.5, 2.0)
    conv_shift = scatter_about(key_list[12], (CONV_CH,), 0.5, 3.0, (), jnp.float32)
    w_proj = scatter_about(key_list[13], (CONV_CH, D), CONV_CH ** -0.5, 0.1875, ((0, 16),))
    return dict(frames=frames, frame_count=frame_count, lookback_mask=lookback_mask, attn_gain=attn_gain, w_query=w_query, w_key=w_key, w_value=w_value, w_out=w_out, conv_gain=conv_gain, w_glu=w_glu, depthwise=depthwise, conv_scale=conv_scale, conv_shift=conv_shift, w_proj=w_proj)


def normalize(x, gain):
    xf = x.astype(jnp.float32)
    mean = lax.optimization_barrier(jnp.mean(xf, axis=-1, keepdims=True))
    centered = xf - mean
    var = lax.optimization_barrier(jnp.mean(centered * centered, axis=-1, keepdims=True))
    return (centered * lax.rsqrt(var + 1e-05) * gain).astype(jnp.bfloat16)

def attend(query_c, keys, values, counts, allowed):
    width = query_c.shape[0]
    pos = jnp.arange(3 * width, dtype=jnp.int32)
    section = pos // width
    place = pos % width
    limit = jnp.where(section == 0, counts[0], jnp.where(section == 1, counts[1], counts[2]))
    block = pos // (width // 2)
    allow = lax.optimization_barrier(jnp.sum((block[:, None] == jnp.arange(4, dtype=jnp.int32)[None, :]) * allowed[None, :], axis=1)) + (block >= 4)
    visible = (place < limit) & (allow > 0)
    factor = 1.0 / math.sqrt(HEAD_DIM)

    def one_head(head):
        start = head * HEAD_DIM
        q_head = lax.dynamic_slice_in_dim(query_c, start, HEAD_DIM, 1)
        k_head = lax.dynamic_slice_in_dim(keys, start, HEAD_DIM, 1)
        v_head = lax.dynamic_slice_in_dim(values, start, HEAD_DIM, 1)
        scores = lax.dot_general(q_head, k_head, (((1,), (1,)), ((), ())), preferred_element_type=jnp.float32) * factor
        scores = jnp.where(visible[None, :], scores, -jnp.inf)
        top = lax.optimization_barrier(jnp.max(scores, axis=1, keepdims=True))
        expo = jnp.exp(scores - top)
        weights = (expo / lax.optimization_barrier(jnp.sum(expo, axis=1, keepdims=True))).astype(jnp.bfloat16)
        return jnp.dot(weights, v_head, preferred_element_type=jnp.float32).astype(jnp.bfloat16)
    stacked = lax.map(one_head, jnp.arange(HEADS, dtype=jnp.int32))
    return jnp.transpose(stacked, (1, 0, 2)).reshape(width, HEADS * HEAD_DIM)

def reference(frames, frame_count, lookback_mask, attn_gain, w_query, w_key, w_value, w_out, conv_gain, w_glu, depthwise, conv_scale, conv_shift, w_proj):
    width = FRAMES_DEV
    norm_a = normalize(frames, attn_gain)
    query = jnp.dot(norm_a, w_query, preferred_element_type=jnp.float32).astype(jnp.bfloat16)
    key = jnp.dot(norm_a, w_key, preferred_element_type=jnp.float32).astype(jnp.bfloat16)
    value = jnp.dot(norm_a, w_value, preferred_element_type=jnp.float32).astype(jnp.bfloat16)
    key_pad = jnp.concatenate([jnp.zeros((2 * width, QKV), jnp.bfloat16), key], axis=0)
    value_pad = jnp.concatenate([jnp.zeros((2 * width, QKV), jnp.bfloat16), value], axis=0)
    count_pad = jnp.concatenate([jnp.zeros((2,), jnp.int32), frame_count.astype(jnp.int32)])

    def span(index):
        start = (index * width).astype(jnp.int32)
        query_c = lax.dynamic_slice_in_dim(query, start, width, 0)
        keys = lax.dynamic_slice_in_dim(key_pad, start, 3 * width, 0)
        values = lax.dynamic_slice_in_dim(value_pad, start, 3 * width, 0)
        counts = lax.dynamic_slice_in_dim(count_pad, index.astype(jnp.int32), 3, 0)
        allowed = lax.dynamic_slice_in_dim(lookback_mask, index.astype(jnp.int32), 1, 0)[0]
        return attend(query_c, keys, values, counts, allowed)
    context = lax.map(span, jnp.arange(SPANS, dtype=jnp.int32)).reshape(FRAMES, QKV)
    mid = (frames.astype(jnp.float32) + jnp.dot(context, w_out, preferred_element_type=jnp.float32)).astype(jnp.bfloat16)
    norm_c = normalize(mid, conv_gain)
    glu_in = jnp.dot(norm_c, w_glu, preferred_element_type=jnp.float32)
    position = jnp.arange(FRAMES, dtype=jnp.int32)
    live = position % width < frame_count[position // width]
    gated = jnp.where(live[:, None], glu_in[:, :CONV_CH] * jax.nn.sigmoid(glu_in[:, CONV_CH:]), 0.0).astype(jnp.bfloat16)
    half = KERNEL // 2
    padded = jnp.pad(gated, ((half, half), (0, 0)))
    conv = jnp.zeros((FRAMES, CONV_CH), jnp.float32)
    for tap in range(KERNEL):
        conv = conv + depthwise[tap] * padded[tap:tap + FRAMES].astype(jnp.float32)
    activated = jax.nn.silu(conv * conv_scale + conv_shift).astype(jnp.bfloat16)
    return (mid.astype(jnp.float32) + jnp.dot(activated, w_proj, preferred_element_type=jnp.float32)).astype(jnp.bfloat16)
```

```python
import functools
import math

import jax
import jax.numpy as jnp
from jax import lax
from jax.experimental import pallas as pl
from jax.experimental.pallas import tpu as pltpu
from jax.sharding import PartitionSpec as P

HEADS = 8
HEAD_DIM = 96
KERNEL = 31


def shifted(block, axis, distance):
    devices = range(lax.axis_size(axis))
    route = [(i - distance, i) for i in devices if i - distance in devices]
    return lax.ppermute(block, axis, route)


def with_halo(value, sides, width):
    for axis, dim in sides:
        size, length = (lax.axis_size(axis), value.shape[dim])
        up = [(i, (i + 1) % size) for i in range(size - 1)]
        down = [(j, i) for i, j in up]
        last = lax.slice_in_dim(value, length - width, length, axis=dim)
        first = lax.slice_in_dim(value, 0, width, axis=dim)
        before = lax.ppermute(last, axis, up)
        after = lax.ppermute(first, axis, down)
        value = jnp.concatenate([before, value, after], axis=dim)
    return value


def normalize(x, gain):
    xf = x.astype(jnp.float32)
    mean = jnp.mean(xf, axis=-1, keepdims=True)
    centered = xf - mean
    var = jnp.mean(centered * centered, axis=-1, keepdims=True)
    return (centered * lax.rsqrt(var + 1e-05) * gain).astype(jnp.bfloat16)


def add_rows(left, piece):
    return jnp.dot(left, piece, preferred_element_type=jnp.float32)


def attend(query_c, keys, values, counts, allowed):
    width = query_c.shape[0]
    pos = jnp.arange(3 * width, dtype=jnp.int32)
    section = pos // width
    place = pos % width
    limit = jnp.where(section == 0, counts[0], jnp.where(section == 1, counts[1], counts[2]))
    block = pos // (width // 2)
    allow = jnp.sum(
        (block[:, None] == jnp.arange(4, dtype=jnp.int32)[None, :]) * allowed[None, :], axis=1
    ) + (block >= 4)
    visible = (place < limit) & (allow > 0)
    factor = 1.0 / math.sqrt(HEAD_DIM)

    def one_head(head):
        start = head * HEAD_DIM
        q_head = lax.dynamic_slice_in_dim(query_c, start, HEAD_DIM, 1)
        k_head = lax.dynamic_slice_in_dim(keys, start, HEAD_DIM, 1)
        v_head = lax.dynamic_slice_in_dim(values, start, HEAD_DIM, 1)
        scores = (
            lax.dot_general(
                q_head, k_head, (((1,), (1,)), ((), ())), preferred_element_type=jnp.float32
            )
            * factor
        )
        scores = jnp.where(visible[None, :], scores, -jnp.inf)
        top = jnp.max(scores, axis=1, keepdims=True)
        expo = jnp.exp(scores - top)
        weights = (expo / jnp.sum(expo, axis=1, keepdims=True)).astype(jnp.bfloat16)
        return jnp.dot(weights, v_head, preferred_element_type=jnp.float32).astype(jnp.bfloat16)

    stacked = lax.map(one_head, jnp.arange(HEADS, dtype=jnp.int32))
    return jnp.transpose(stacked, (1, 0, 2)).reshape(width, HEADS * HEAD_DIM)


def plain(
    frames,
    frame_count,
    lookback_mask,
    attn_gain,
    w_query,
    w_key,
    w_value,
    w_out,
    conv_gain,
    w_glu,
    depthwise,
    conv_scale,
    conv_shift,
    w_proj,
):
    width = frames.shape[0]
    conv_width = w_proj.shape[0] * lax.axis_size("tm")
    norm_a = normalize(frames, attn_gain)
    query = add_rows(norm_a, lax.all_gather(w_query, "tm", axis=0, tiled=True))
    key = add_rows(norm_a, lax.all_gather(w_key, "tm", axis=0, tiled=True))
    value = add_rows(norm_a, lax.all_gather(w_value, "tm", axis=0, tiled=True))
    query = query.astype(jnp.bfloat16)
    key = key.astype(jnp.bfloat16)
    value = value.astype(jnp.bfloat16)
    own = (key, value, frame_count)
    received = []
    current = own
    for step in range(2):
        current = shifted((current[0], current[1], current[2]), "tm", 1)
        received.append(current)
    nearer, farther = (received[0], received[1])
    keys = jnp.concatenate([farther[0], nearer[0], key], axis=0)
    values = jnp.concatenate([farther[1], nearer[1], value], axis=0)
    counts = jnp.concatenate([farther[2], nearer[2], frame_count])
    context = attend(query, keys, values, counts, lookback_mask[0])
    attn_sum = add_rows(context, lax.all_gather(w_out, "tm", axis=0, tiled=True))
    mid = (frames.astype(jnp.float32) + attn_sum).astype(jnp.bfloat16)
    norm_c = normalize(mid, conv_gain)
    glu_in = add_rows(norm_c, lax.all_gather(w_glu, "tm", axis=0, tiled=True))
    live = jnp.arange(width, dtype=jnp.int32) < frame_count[0]
    gated = jnp.where(
        live[:, None], glu_in[:, :conv_width] * jax.nn.sigmoid(glu_in[:, conv_width:]), 0.0
    ).astype(jnp.bfloat16)
    half = KERNEL // 2
    padded = with_halo(gated, (("tm", 0),), half)
    conv = jnp.zeros((width, conv_width), jnp.float32)
    for tap in range(KERNEL):
        conv = conv + depthwise[tap] * padded[tap : tap + width].astype(jnp.float32)
    activated = jax.nn.silu(conv * conv_scale + conv_shift).astype(jnp.bfloat16)
    conv_sum = add_rows(activated, lax.all_gather(w_proj, "tm", axis=0, tiled=True))
    return (mid.astype(jnp.float32) + conv_sum).astype(jnp.bfloat16)


F32 = jnp.float32
BF16 = jnp.bfloat16
MESH = pl.DeviceIdType.MESH
TILE = 256


def norm_rows(source, gain_ref, target):
    rows = source.shape[0]

    @pl.loop(0, rows // 32)
    def _(step):
        at = pl.ds(pl.multiple_of(step * 32, 32), 32)
        xf = source[at, :].astype(F32)
        mean = jnp.mean(xf, axis=-1, keepdims=True)
        centered = xf - mean
        var = jnp.mean(centered * centered, axis=-1, keepdims=True)
        target[at, :] = (centered * lax.rsqrt(var + 1e-05) * gain_ref[...]).astype(BF16)


def block(
    n,
    frames_ref, count_ref, look_ref, gain_a_ref, wq_ref, wk_ref, wv_ref, wo_ref, gain_c_ref,
    wg_ref, taps_ref, scale_ref, shift_ref, wp_ref,
    out_ref,
    w_qkv, w_out, w_glu, w_proj, norm, counts, q_s, kv_s, ctx_s, mid_s, normc_s, gpad, act_s,
    hsend, hrecv,
    ring_send, ring_recv, x_send, x_recv, c_send, c_recv, n_send, n_recv, m_send, m_recv,
    h_send, h_recv,
):
    g = lax.axis_index("groups")
    t = lax.axis_index("tm")
    core = lax.rem(t, 2)
    chip = t // 2
    chips = n // 2
    deep = chips // 2
    hops_a, hops_b = chips // 2, chips // 2 - 1
    place = jnp.where(lax.rem(chip, 2) == 0, chip // 2, chips - 1 - chip // 2)
    turn = 1 - 2 * core

    def at_place(r):
        r = lax.rem(r + 2 * chips, chips)
        q = jnp.where(r < deep, 2 * r, 2 * (chips - 1 - r) + 1)
        return 2 * q + core

    next_a, next_b = at_place(place + turn), at_place(place - turn)
    pair = t + turn
    here = lambda index: (g, index)
    across = (1 - g, t)

    weights = (w_qkv, w_out, w_glu, w_proj)
    depth = tuple(w.shape[0] // n for w in weights)
    third = tuple(d // 48 * 16 for d in depth)

    def rows(w, owner, start, size):
        return weights[w].at[pl.ds(pl.multiple_of(owner * depth[w] + start, 16), size), :]

    def copy(src, dst, send, recv, device):
        return pltpu.make_async_remote_copy(
            src_ref=src, dst_ref=dst, send_sem=send, recv_sem=recv,
            device_id=device, device_id_type=MESH,
        )

    def ring(w, side, hop):
        sign = turn if side == 0 else -turn
        view = rows(w, at_place(place - sign * hop), g * third[w], depth[w] - third[w])
        slot = hop + side * hops_a
        target = next_a if side == 0 else next_b
        return copy(view, view, ring_send.at[w, slot], ring_recv.at[w, slot], here(target))

    def arrived(side, hop):
        return at_place(place - (turn if side == 0 else -turn) * (hop + 1))

    def over_x(w, side, hop):
        view = rows(w, arrived(side, hop), g * (depth[w] - third[w]), third[w])
        slot = hop + side * hops_a
        return copy(view, view, x_send.at[w, slot], x_recv.at[w, slot], across)

    def over_core(w, slot, owner):
        view = rows(w, owner, 0, depth[w])
        return copy(view, view, c_send.at[w, slot], c_recv.at[w, slot], here(pair))

    sides = ((0, hops_a), (1, hops_b))

    def begin(w):
        ring(w, 0, 0).start()
        ring(w, 1, 0).start()
        over_core(w, chips - 1, t).start()

    def step(w, hop):
        for side, hops in sides:
            if hop < hops:
                ring(w, side, hop).wait_recv()
                if hop + 1 < hops:
                    ring(w, side, hop + 1).start()
                over_x(w, side, hop).start()

    def spread(w, hop):
        for side, hops in sides:
            if hop < hops:
                over_x(w, side, hop).wait_recv()
                over_core(w, hop + side * hops_a, arrived(side, hop)).start()

    def ready(w):
        for slot in range(chips):
            over_core(w, slot, t).wait_recv()

    barrier = pltpu.get_barrier_semaphore()
    around = [lax.rem(t + n + d, n) for d in (1, -1, 2, -2)]
    for device in [here(i) for i in (next_a, next_b, pair, *around)] + [across]:
        pl.semaphore_signal(barrier, inc=1, device_id=device, device_id_type=MESH)

    own = lambda w: pl.ds(pl.multiple_of(t * depth[w], 16), depth[w])
    width = wq_ref.shape[1]
    w_qkv[own(0), 0:width] = wq_ref[...]
    w_qkv[own(0), width : 2 * width] = wk_ref[...]
    w_qkv[own(0), 2 * width : 3 * width] = wv_ref[...]
    w_out[own(1), :] = wo_ref[...]
    w_glu[own(2), :] = wg_ref[...]
    w_proj[own(3), :] = wp_ref[...]
    pl.semaphore_wait(barrier, 8)
    begin(0)
    begin(1)

    length = frames_ref.shape[0]
    part = lambda i: norm.at[pl.ds(i * length, length), :]
    norm_rows(frames_ref, gain_a_ref, part(2))
    counts[2] = count_ref[...]
    near = copy(part(2), part(1), n_send.at[0], n_recv.at[0], here(t + 1))
    far = copy(part(2), part(0), n_send.at[1], n_recv.at[1], here(t + 2))
    relay = copy(part(1), part(0), n_send.at[2], n_recv.at[1], here(t + 1))
    near_count = copy(counts.at[2], counts.at[1], m_send.at[0], m_recv.at[0], here(t + 1))
    far_count = copy(counts.at[2], counts.at[0], m_send.at[1], m_recv.at[1], here(t + 2))
    even = core == 0

    @pl.when(t + 1 < n)
    def _():
        near.start()
        near_count.start()

    @pl.when(t + 2 < n)
    def _():
        far_count.start()

    @pl.when((t + 2 < n) & even)
    def _():
        far.start()

    @pl.when(t < 2)
    def _():
        norm[0:length, :] = jnp.zeros((length, norm.shape[1]), BF16)
        counts[0] = jnp.zeros(counts.shape[1:], jnp.int32)

    @pl.when(t < 1)
    def _():
        norm[length : 2 * length, :] = jnp.zeros((length, norm.shape[1]), BF16)
        counts[1] = jnp.zeros(counts.shape[1:], jnp.int32)

    ctx_s[...] = jnp.zeros_like(ctx_s)

    step(0, 0)
    step(1, 0)

    @pl.when(t >= 1)
    def _():
        near.wait_recv()
        near_count.wait_recv()

    @pl.when((t >= 1) & even)
    def _():
        relay.start()

    for hop in range(1, hops_a):
        step(0, hop)
        spread(0, hop - 1)
        step(1, hop)
        spread(1, hop - 1)
        if hop == hops_a - 2:
            begin(2)
            begin(3)
    spread(0, hops_a - 1)

    @pl.when(t >= 2)
    def _():
        far.wait_recv()
        far_count.wait_recv()

    ready(0)
    spread(1, hops_a - 1)

    @pl.loop(0, width // TILE)
    def _(j):
        cols = pl.ds(pl.multiple_of(j * TILE, TILE), TILE)
        q_s[:, cols] = jnp.dot(
            norm[2 * length : 3 * length, :], w_qkv[:, cols], preferred_element_type=F32
        ).astype(BF16)

    step(2, 0)
    step(3, 0)

    @pl.loop(0, 2 * width // TILE)
    def _(j):
        cols = pl.ds(pl.multiple_of(j * TILE, TILE), TILE)
        source = pl.ds(pl.multiple_of(j * TILE + width, TILE), TILE)
        kv_s[:, cols] = jnp.dot(norm[...], w_qkv[:, source], preferred_element_type=F32).astype(
            BF16
        )

    step(2, 1)
    step(3, 1)
    spread(2, 0)
    spread(3, 0)

    lane = lax.broadcasted_iota(jnp.int32, (8, length), 1)
    repeat = lambda v: jnp.concatenate([v] * (length // v.shape[1]), axis=1)
    limits = [repeat(counts[i]) for i in range(3)]
    seen = [
        (lane < limits[0]) & (look_ref[:, 0:length] > 0),
        (lane < limits[1]) & (look_ref[:, length : 2 * length] > 0),
        lane < limits[2],
    ]
    hide = jnp.concatenate([jnp.where(s, 0.0, -1e30) for s in seen], axis=1)[0:1, :]
    factor = math.log2(math.e) / math.sqrt(HEAD_DIM)

    for head in range(HEADS):
        first = head * HEAD_DIM
        lo = first // 128 * 128
        hi = -(-(first + HEAD_DIM) // 128) * 128
        inside = lax.broadcasted_iota(jnp.int32, (length, hi - lo), 1) + lo
        inside = (inside >= first) & (inside < first + HEAD_DIM)
        q_head = jnp.where(inside, q_s[:, lo:hi].astype(F32), 0.0).astype(BF16)
        scores = lax.dot_general(
            q_head, kv_s[:, lo:hi], (((1,), (1,)), ((), ())), preferred_element_type=F32
        )
        scores = scores * factor + hide
        top = jnp.max(scores, axis=1, keepdims=True)
        expo = jnp.exp2(scores - top)
        total = jnp.sum(expo, axis=1, keepdims=True)
        context = jnp.dot(
            expo.astype(BF16), kv_s[:, width + lo : width + hi], preferred_element_type=F32
        )
        context = context / total
        ctx_s[:, lo:hi] = jnp.where(inside, context, ctx_s[:, lo:hi].astype(F32)).astype(BF16)
        if head % 2 == 1 and head // 2 + 2 < hops_a:
            hop = head // 2 + 2
            step(2, hop)
            spread(2, hop - 1)
            step(3, hop)
            spread(3, hop - 1)
    for hop in range(HEADS // 2 + 2, hops_a):
        step(2, hop)
        spread(2, hop - 1)
        step(3, hop)
        spread(3, hop - 1)
    ready(1)

    @pl.loop(0, mid_s.shape[1] // TILE)
    def _(j):
        cols = pl.ds(pl.multiple_of(j * TILE, TILE), TILE)
        add = jnp.dot(ctx_s[...], w_out[:, cols], preferred_element_type=F32)
        mid_s[:, cols] = (frames_ref[:, cols].astype(F32) + add).astype(BF16)

    spread(2, hops_a - 1)
    norm_rows(mid_s, gain_c_ref, normc_s)
    spread(3, hops_a - 1)
    ready(2)

    half_width = w_glu.shape[1] // 2
    live = lax.broadcasted_iota(jnp.int32, (length, 1), 0) < count_ref[0:1, 0:1]

    @pl.loop(0, half_width // TILE)
    def _(j):
        cols = pl.ds(pl.multiple_of(j * TILE, TILE), TILE)
        gate_cols = pl.ds(pl.multiple_of(j * TILE + half_width, TILE), TILE)
        left = jnp.dot(normc_s[...], w_glu[:, cols], preferred_element_type=F32)
        gate = jnp.dot(normc_s[...], w_glu[:, gate_cols], preferred_element_type=F32)
        gated = jnp.where(live, left * jax.nn.sigmoid(gate), 0.0).astype(BF16)
        gpad[16 : 16 + length, cols] = gated.astype(F32)
        hsend[0, :, cols] = gated[0:16]
        hsend[1, :, cols] = gated[length - 16 : length]

    below = copy(hsend.at[1], hrecv.at[0], h_send.at[0], h_recv.at[0], here(t + 1))
    above = copy(hsend.at[0], hrecv.at[1], h_send.at[1], h_recv.at[1], here(t - 1))

    @pl.when(t + 1 < n)
    def _():
        below.start()

    @pl.when(t >= 1)
    def _():
        above.start()

    @pl.when(t >= 1)
    def _():
        below.wait_recv()
        gpad[0:16, :] = hrecv[0].astype(F32)

    @pl.when(t < 1)
    def _():
        gpad[0:16, :] = jnp.zeros((16, half_width), F32)

    @pl.when(t + 1 < n)
    def _():
        above.wait_recv()
        gpad[16 + length : 32 + length, :] = hrecv[1].astype(F32)

    @pl.when(t + 1 >= n)
    def _():
        gpad[16 + length : 32 + length, :] = jnp.zeros((16, half_width), F32)

    strip = 128

    @pl.loop(0, half_width // 128)
    def _(j):
        cols = pl.ds(pl.multiple_of(j * 128, 128), 128)
        for start in range(0, length, strip):
            conv = jnp.zeros((strip, 128), F32)
            for shift in range(8):
                moved = gpad[start + shift : start + shift + strip + 24, cols]
                for at in range(shift, 32, 8):
                    if at >= 1:
                        conv = conv + taps_ref[at - 1 : at, cols] * moved[at - shift : at - shift + strip]
            pre = conv * scale_ref[:, cols] + shift_ref[:, cols]
            act_s[start : start + strip, cols] = (pre * jax.nn.sigmoid(pre)).astype(BF16)

    ready(3)

    @pl.loop(0, out_ref.shape[1] // TILE)
    def _(j):
        cols = pl.ds(pl.multiple_of(j * TILE, TILE), TILE)
        add = jnp.dot(act_s[...], w_proj[:, cols], preferred_element_type=F32)
        out_ref[:, cols] = (mid_s[:, cols].astype(F32) + add).astype(BF16)

    for w in range(4):
        for side, hops in sides:
            for hop in range(hops):
                ring(w, side, hop).wait_send()
                over_x(w, side, hop).wait_send()
        for slot in range(chips):
            over_core(w, slot, t).wait_send()

    @pl.when(t + 1 < n)
    def _():
        near.wait_send()
        near_count.wait_send()
        below.wait_send()

    @pl.when(t >= 1)
    def _():
        above.wait_send()

    @pl.when(t + 2 < n)
    def _():
        far_count.wait_send()

    @pl.when((t + 2 < n) & even)
    def _():
        far.wait_send()

    @pl.when((t >= 1) & even)
    def _():
        relay.wait_send()


def fused(
    n, frames, frame_count, lookback_mask, attn_gain, w_query, w_key, w_value, w_out, conv_gain,
    w_glu, depthwise, conv_scale, conv_shift, w_proj,
):
    length, model = frames.shape
    width = w_query.shape[1]
    half = w_glu.shape[1] // 2
    chips = n // 2
    count = jnp.broadcast_to(frame_count.reshape(1, 1), (8, 128))
    look = jnp.broadcast_to(jnp.repeat(lookback_mask, length // 2, axis=1), (8, 2 * length))
    dma = pltpu.SemaphoreType.DMA
    params = 3 * width * model + model * width + 2 * half * model + half * model
    return pl.pallas_call(
        functools.partial(block, n),
        out_shape=jax.ShapeDtypeStruct((length, model), BF16),
        in_specs=[pl.BlockSpec(memory_space=pltpu.VMEM)] * 14,
        out_specs=pl.BlockSpec(memory_space=pltpu.VMEM),
        scratch_shapes=[
            pltpu.VMEM((model, 3 * width), BF16),
            pltpu.VMEM((width, model), BF16),
            pltpu.VMEM((model, 2 * half), BF16),
            pltpu.VMEM((half, model), BF16),
            pltpu.VMEM((3 * length, model), BF16),
            pltpu.VMEM((3, 8, 128), jnp.int32),
            pltpu.VMEM((length, width), BF16),
            pltpu.VMEM((3 * length, 2 * width), BF16),
            pltpu.VMEM((length, width), BF16),
            pltpu.VMEM((length, model), BF16),
            pltpu.VMEM((length, model), BF16),
            pltpu.VMEM((length + 32, half), F32),
            pltpu.VMEM((length, half), BF16),
            pltpu.VMEM((2, 16, half), BF16),
            pltpu.VMEM((2, 16, half), BF16),
            dma((4, chips - 1)), dma((4, chips - 1)),
            dma((4, chips - 1)), dma((4, chips - 1)),
            dma((4, chips)), dma((4, chips)),
            dma((3,)), dma((2,)), dma((2,)), dma((2,)), dma((2,)), dma((2,)),
        ],
        compiler_params=pltpu.CompilerParams(
            collective_id=0, has_side_effects=True, vmem_limit_bytes=56 * 1024 * 1024
        ),
        cost_estimate=pl.CostEstimate(
            flops=2 * length * params, bytes_accessed=2 * params, transcendentals=length * half
        ),
    )(
        frames, count, look, attn_gain.reshape(1, -1), w_query, w_key, w_value, w_out,
        conv_gain.reshape(1, -1), w_glu, depthwise, conv_scale.reshape(1, -1),
        conv_shift.reshape(1, -1), w_proj,
    )


def shards(groups, *args):
    n = lax.axis_size("tm")
    frames, w_query, w_out, w_glu, w_proj = args[0], args[4], args[7], args[9], args[13]
    whole = all(w.shape[0] % 16 == 0 and w.shape[0] >= 48 for w in (w_query, w_out, w_glu, w_proj))
    tiles = all(
        w.shape[1] % TILE == 0 for w in (w_query, w_out, w_proj)
    ) and w_glu.shape[1] % (2 * TILE) == 0
    if groups == 2 and n % 8 == 0 and whole and tiles and frames.shape[0] % 256 == 0:
        return fused(n, *args)
    return plain(*args)


def solution(mesh):
    return jax.shard_map(
        functools.partial(shards, mesh.shape["groups"]),
        mesh=mesh,
        in_specs=(
            P(("groups", "tm"), None),
            P(("groups", "tm")),
            P(("groups", "tm"), None),
            P(),
            P("tm", None),
            P("tm", None),
            P("tm", None),
            P("tm", None),
            P(),
            P("tm", None),
            P(),
            P(),
            P(),
            P("tm", None),
        ),
        out_specs=P(("groups", "tm"), None),
        check_vma=False,
    )
```

```python
import functools
import math

import jax
import jax.numpy as jnp
from jax import lax
from jax.experimental import pallas as pl
from jax.experimental.pallas import tpu as pltpu
from jax.sharding import PartitionSpec as P

HEADS = 8
HEAD_DIM = 96
KERNEL = 31


def shifted(block, axis, distance):
    devices = range(lax.axis_size(axis))
    route = [(i - distance, i) for i in devices if i - distance in devices]
    return lax.ppermute(block, axis, route)


def with_halo(value, sides, width):
    for axis, dim in sides:
        size, length = (lax.axis_size(axis), value.shape[dim])
        up = [(i, (i + 1) % size) for i in range(size - 1)]
        down = [(j, i) for i, j in up]
        last = lax.slice_in_dim(value, length - width, length, axis=dim)
        first = lax.slice_in_dim(value, 0, width, axis=dim)
        before = lax.ppermute(last, axis, up)
        after = lax.ppermute(first, axis, down)
        value = jnp.concatenate([before, value, after], axis=dim)
    return value


def normalize(x, gain):
    xf = x.astype(jnp.float32)
    mean = jnp.mean(xf, axis=-1, keepdims=True)
    centered = xf - mean
    var = jnp.mean(centered * centered, axis=-1, keepdims=True)
    return (centered * lax.rsqrt(var + 1e-05) * gain).astype(jnp.bfloat16)


def add_rows(left, piece):
    return jnp.dot(left, piece, preferred_element_type=jnp.float32)


def attend(query_c, keys, values, counts, allowed):
    width = query_c.shape[0]
    pos = jnp.arange(3 * width, dtype=jnp.int32)
    section = pos // width
    place = pos % width
    limit = jnp.where(section == 0, counts[0], jnp.where(section == 1, counts[1], counts[2]))
    block = pos // (width // 2)
    allow = jnp.sum(
        (block[:, None] == jnp.arange(4, dtype=jnp.int32)[None, :]) * allowed[None, :], axis=1
    ) + (block >= 4)
    visible = (place < limit) & (allow > 0)
    factor = 1.0 / math.sqrt(HEAD_DIM)

    def one_head(head):
        start = head * HEAD_DIM
        q_head = lax.dynamic_slice_in_dim(query_c, start, HEAD_DIM, 1)
        k_head = lax.dynamic_slice_in_dim(keys, start, HEAD_DIM, 1)
        v_head = lax.dynamic_slice_in_dim(values, start, HEAD_DIM, 1)
        scores = (
            lax.dot_general(
                q_head, k_head, (((1,), (1,)), ((), ())), preferred_element_type=jnp.float32
            )
            * factor
        )
        scores = jnp.where(visible[None, :], scores, -jnp.inf)
        top = jnp.max(scores, axis=1, keepdims=True)
        expo = jnp.exp(scores - top)
        weights = (expo / jnp.sum(expo, axis=1, keepdims=True)).astype(jnp.bfloat16)
        return jnp.dot(weights, v_head, preferred_element_type=jnp.float32).astype(jnp.bfloat16)

    stacked = lax.map(one_head, jnp.arange(HEADS, dtype=jnp.int32))
    return jnp.transpose(stacked, (1, 0, 2)).reshape(width, HEADS * HEAD_DIM)


def plain(
    frames,
    frame_count,
    lookback_mask,
    attn_gain,
    w_query,
    w_key,
    w_value,
    w_out,
    conv_gain,
    w_glu,
    depthwise,
    conv_scale,
    conv_shift,
    w_proj,
):
    width = frames.shape[0]
    conv_width = w_proj.shape[0] * lax.axis_size("tm")
    norm_a = normalize(frames, attn_gain)
    query = add_rows(norm_a, lax.all_gather(w_query, "tm", axis=0, tiled=True))
    key = add_rows(norm_a, lax.all_gather(w_key, "tm", axis=0, tiled=True))
    value = add_rows(norm_a, lax.all_gather(w_value, "tm", axis=0, tiled=True))
    query = query.astype(jnp.bfloat16)
    key = key.astype(jnp.bfloat16)
    value = value.astype(jnp.bfloat16)
    own = (key, value, frame_count)
    received = []
    current = own
    for step in range(2):
        current = shifted((current[0], current[1], current[2]), "tm", 1)
        received.append(current)
    nearer, farther = (received[0], received[1])
    keys = jnp.concatenate([farther[0], nearer[0], key], axis=0)
    values = jnp.concatenate([farther[1], nearer[1], value], axis=0)
    counts = jnp.concatenate([farther[2], nearer[2], frame_count])
    context = attend(query, keys, values, counts, lookback_mask[0])
    attn_sum = add_rows(context, lax.all_gather(w_out, "tm", axis=0, tiled=True))
    mid = (frames.astype(jnp.float32) + attn_sum).astype(jnp.bfloat16)
    norm_c = normalize(mid, conv_gain)
    glu_in = add_rows(norm_c, lax.all_gather(w_glu, "tm", axis=0, tiled=True))
    live = jnp.arange(width, dtype=jnp.int32) < frame_count[0]
    gated = jnp.where(
        live[:, None], glu_in[:, :conv_width] * jax.nn.sigmoid(glu_in[:, conv_width:]), 0.0
    ).astype(jnp.bfloat16)
    half = KERNEL // 2
    padded = with_halo(gated, (("tm", 0),), half)
    conv = jnp.zeros((width, conv_width), jnp.float32)
    for tap in range(KERNEL):
        conv = conv + depthwise[tap] * padded[tap : tap + width].astype(jnp.float32)
    activated = jax.nn.silu(conv * conv_scale + conv_shift).astype(jnp.bfloat16)
    conv_sum = add_rows(activated, lax.all_gather(w_proj, "tm", axis=0, tiled=True))
    return (mid.astype(jnp.float32) + conv_sum).astype(jnp.bfloat16)


F32 = jnp.float32
BF16 = jnp.bfloat16
MESH = pl.DeviceIdType.MESH
TILE = 256


def norm_rows(source, gain_ref, target):
    rows = source.shape[0]

    @pl.loop(0, rows // 32)
    def _(step):
        at = pl.ds(pl.multiple_of(step * 32, 32), 32)
        xf = source[at, :].astype(F32)
        mean = jnp.mean(xf, axis=-1, keepdims=True)
        centered = xf - mean
        var = jnp.mean(centered * centered, axis=-1, keepdims=True)
        target[at, :] = (centered * lax.rsqrt(var + 1e-05) * gain_ref[...].reshape(1, -1)).astype(BF16)


def block(
    n,
    frames_ref, count_ref, look_ref, gain_a_ref, wq_ref, wk_ref, wv_ref, wo_ref, gain_c_ref,
    wg_ref, taps_ref, scale_ref, shift_ref, wp_ref,
    out_ref,
    w_qkv, w_out, w_glu, w_proj, norm, counts, q_s, kv_s, ctx_s, mid_s, normc_s, gpad, act_s,
    hsend, hrecv,
    ring_send, ring_recv, x_send, x_recv, c_send, c_recv, n_send, n_recv, m_send, m_recv,
    h_send, h_recv,
):
    g = lax.axis_index("groups")
    t = lax.axis_index("tm")
    core = lax.rem(t, 2)
    chip = t // 2
    chips = n // 2
    deep = chips // 2
    hops_a, hops_b = chips // 2, chips // 2 - 1
    place = jnp.where(lax.rem(chip, 2) == 0, chip // 2, chips - 1 - chip // 2)
    turn = 1 - 2 * core

    def at_place(r):
        r = lax.rem(r + 2 * chips, chips)
        q = jnp.where(r < deep, 2 * r, 2 * (chips - 1 - r) + 1)
        return 2 * q + core

    next_a, next_b = at_place(place + turn), at_place(place - turn)
    pair = t + turn
    here = lambda index: (g, index)
    across = (1 - g, t)

    weights = (w_qkv, w_out, w_glu, w_proj)
    depth = tuple(w.shape[0] // n for w in weights)
    full = tuple(w.shape[1] for w in weights)
    around_cols = tuple((61 * c + 6400) // 12800 * 128 for c in full)
    pieces = tuple(
        (w, start, size)
        for w, parts in enumerate((2, 1, 2, 1))
        for size in [depth[w] // parts if depth[w] % (16 * parts) == 0 else depth[w]]
        for start in range(0, depth[w], size)
    )

    def rows(p, owner, start, size):
        w, low, high = pieces[p]
        at = pl.ds(pl.multiple_of(owner * depth[w] + low, 16), high)
        return weights[w].at[at, pl.ds(pl.multiple_of(start, 128), size)]

    def sizes(p):
        w = pieces[p][0]
        return full[w], around_cols[w]

    def copy(src, dst, send, recv, device):
        return pltpu.make_async_remote_copy(
            src_ref=src, dst_ref=dst, send_sem=send, recv_sem=recv,
            device_id=device, device_id_type=MESH,
        )

    def ring(w, side, hop):
        sign = turn if side == 0 else -turn
        cols, ringed = sizes(w)
        view = rows(w, at_place(place - sign * hop), g * (cols - ringed), ringed)
        slot = hop + side * hops_a
        target = next_a if side == 0 else next_b
        return copy(view, view, ring_send.at[w, slot], ring_recv.at[w, slot], here(target))

    def arrived(side, hop):
        return at_place(place - (turn if side == 0 else -turn) * (hop + 1))

    def over_x(w, side, hop):
        cols, ringed = sizes(w)
        view = rows(w, arrived(side, hop), g * ringed, cols - ringed)
        slot = hop + side * hops_a
        return copy(view, view, x_send.at[w, slot], x_recv.at[w, slot], across)

    def over_core(w, slot, owner):
        view = rows(w, owner, 0, sizes(w)[0])
        return copy(view, view, c_send.at[w, slot], c_recv.at[w, slot], here(pair))

    sides = ((0, hops_a), (1, hops_b))

    def begin(w):
        ring(w, 0, 0).start()
        ring(w, 1, 0).start()
        over_core(w, chips - 1, t).start()

    stepped, spreaded, rounds = set(), set(), []

    def step(w, hop):
        stepped.add((w, hop))
        for side, hops in sides:
            if hop < hops:
                ring(w, side, hop).wait_recv()
                if hop + 1 < hops:
                    ring(w, side, hop + 1).start()
                over_x(w, side, hop).start()

    def spread(w, hop):
        if (w, hop) in spreaded:
            return
        spreaded.add((w, hop))
        for side, hops in sides:
            if hop < hops:
                over_x(w, side, hop).wait_recv()
                over_core(w, hop + side * hops_a, arrived(side, hop)).start()

    turns = (0, 0, 2, 3, 4, 5)

    def advance():
        number = len(rounds)
        rounds.append(number)
        for p, first in enumerate(turns):
            hop = number - first - 1
            if hop == -1:
                begin(p)
            if 0 <= hop < hops_a:
                step(p, hop)
            if 0 < hop <= hops_a:
                spread(p, hop - 1)

    def finish(w):
        for p, piece in enumerate(pieces):
            if piece[0] == w:
                while (p, hops_a - 1) not in stepped:
                    advance()
        for p, piece in enumerate(pieces):
            if piece[0] == w:
                spread(p, hops_a - 1)

    def ready(w):
        finish(w)
        for p, piece in enumerate(pieces):
            if piece[0] == w:
                for slot in range(chips):
                    over_core(p, slot, t).wait_recv()

    barrier = pltpu.get_barrier_semaphore()
    around = [lax.rem(t + n + d, n) for d in (1, -1, 2, -2)]
    for device in [here(i) for i in (next_a, next_b, pair, *around)] + [across]:
        pl.semaphore_signal(barrier, inc=1, device_id=device, device_id_type=MESH)

    own = lambda w: pl.ds(pl.multiple_of(t * depth[w], 16), depth[w])
    width = wq_ref.shape[1]
    w_qkv[own(0), 0:width] = wq_ref[...]
    w_qkv[own(0), width : 2 * width] = wk_ref[...]
    w_qkv[own(0), 2 * width : 3 * width] = wv_ref[...]
    w_out[own(1), :] = wo_ref[...]
    w_glu[own(2), :] = wg_ref[...]
    w_proj[own(3), :] = wp_ref[...]
    pl.semaphore_wait(barrier, 8)
    advance()

    length = frames_ref.shape[0]
    part = lambda i: norm.at[pl.ds(i * length, length), :]
    norm_rows(frames_ref, gain_a_ref, part(2))
    counts[2] = jnp.full(counts.shape[1:], count_ref[0], jnp.int32)
    near = copy(part(2), part(1), n_send.at[0], n_recv.at[0], here(t + 1))
    far = copy(part(2), part(0), n_send.at[1], n_recv.at[1], here(t + 2))
    relay = copy(part(1), part(0), n_send.at[2], n_recv.at[1], here(t + 1))
    near_count = copy(counts.at[2], counts.at[1], m_send.at[0], m_recv.at[0], here(t + 1))
    far_count = copy(counts.at[2], counts.at[0], m_send.at[1], m_recv.at[1], here(t + 2))
    even = core == 0

    @pl.when(t + 1 < n)
    def _():
        near.start()
        near_count.start()

    @pl.when(t + 2 < n)
    def _():
        far_count.start()

    @pl.when((t + 2 < n) & even)
    def _():
        far.start()

    @pl.when(t < 2)
    def _():
        norm[0:length, :] = jnp.zeros((length, norm.shape[1]), BF16)
        counts[0] = jnp.zeros(counts.shape[1:], jnp.int32)

    @pl.when(t < 1)
    def _():
        norm[length : 2 * length, :] = jnp.zeros((length, norm.shape[1]), BF16)
        counts[1] = jnp.zeros(counts.shape[1:], jnp.int32)

    ctx_s[...] = jnp.zeros_like(ctx_s)

    advance()

    @pl.when(t >= 1)
    def _():
        near.wait_recv()
        near_count.wait_recv()

    @pl.when((t >= 1) & even)
    def _():
        relay.start()

    finish(0)

    @pl.when(t >= 2)
    def _():
        far.wait_recv()
        far_count.wait_recv()

    ready(0)

    @pl.loop(0, width // TILE)
    def _(j):
        cols = pl.ds(pl.multiple_of(j * TILE, TILE), TILE)
        q_s[:, cols] = jnp.dot(
            norm[2 * length : 3 * length, :], w_qkv[:, cols], preferred_element_type=F32
        ).astype(BF16)

    def spans(base):
        @pl.loop(0, width // TILE)
        def _(j):
            cols = pl.ds(pl.multiple_of(base + j * TILE, TILE), TILE)
            source = pl.ds(pl.multiple_of(base + width + j * TILE, TILE), TILE)
            kv_s[:, cols] = jnp.dot(
                norm[...], w_qkv[:, source], preferred_element_type=F32
            ).astype(BF16)

    spans(0)
    advance()
    spans(width)

    lane = lax.broadcasted_iota(jnp.int32, (1, 128), 1)
    hide = []
    for b in range(3 * length // 128):
        limit = counts[b * 128 // length][0:1, :] - b * 128 % length
        seen = lane < limit
        if b * 128 < 2 * length:
            seen = seen & (jnp.full((1, 128), look_ref[0, b * 128 // (length // 2)], jnp.int32) > 0)
        hide.append(jnp.where(seen, 0.0, -1e30))
    hide = jnp.concatenate(hide, axis=1)
    factor = math.log2(math.e) / math.sqrt(HEAD_DIM)

    for head in range(HEADS):
        first = head * HEAD_DIM
        lo = first // 128 * 128
        hi = -(-(first + HEAD_DIM) // 128) * 128
        inside = lax.broadcasted_iota(jnp.int32, (length, hi - lo), 1) + lo
        inside = (inside >= first) & (inside < first + HEAD_DIM)
        q_head = jnp.where(inside, q_s[:, lo:hi].astype(F32), 0.0).astype(BF16)
        scores = lax.dot_general(
            q_head, kv_s[:, lo:hi], (((1,), (1,)), ((), ())), preferred_element_type=F32
        )
        scores = scores * factor + hide
        top = jnp.max(scores, axis=1, keepdims=True)
        expo = jnp.exp2(scores - top)
        total = jnp.sum(expo, axis=1, keepdims=True)
        context = jnp.dot(
            expo.astype(BF16), kv_s[:, width + lo : width + hi], preferred_element_type=F32
        )
        context = context / total
        ctx_s[:, lo:hi] = jnp.where(inside, context, ctx_s[:, lo:hi].astype(F32)).astype(BF16)
        if head == 1:
            advance()
        if head == 6:
            advance()
    ready(1)

    @pl.loop(0, mid_s.shape[1] // TILE)
    def _(j):
        cols = pl.ds(pl.multiple_of(j * TILE, TILE), TILE)
        add = jnp.dot(ctx_s[...], w_out[:, cols], preferred_element_type=F32)
        mid_s[:, cols] = (frames_ref[:, cols].astype(F32) + add).astype(BF16)

    norm_rows(mid_s, gain_c_ref, normc_s)
    ready(2)

    half_width = w_glu.shape[1] // 2
    live = lax.broadcasted_iota(jnp.int32, (length, 1), 0) < count_ref[0]

    @pl.loop(0, half_width // TILE)
    def _(j):
        cols = pl.ds(pl.multiple_of(j * TILE, TILE), TILE)
        gate_cols = pl.ds(pl.multiple_of(j * TILE + half_width, TILE), TILE)
        left = jnp.dot(normc_s[...], w_glu[:, cols], preferred_element_type=F32)
        gate = jnp.dot(normc_s[...], w_glu[:, gate_cols], preferred_element_type=F32)
        gated = jnp.where(live, left * jax.nn.sigmoid(gate), 0.0).astype(BF16)
        gpad[16 : 16 + length, cols] = gated.astype(F32)
        hsend[0, :, cols] = gated[0:16]
        hsend[1, :, cols] = gated[length - 16 : length]

    below = copy(hsend.at[1], hrecv.at[0], h_send.at[0], h_recv.at[0], here(t + 1))
    above = copy(hsend.at[0], hrecv.at[1], h_send.at[1], h_recv.at[1], here(t - 1))

    @pl.when(t + 1 < n)
    def _():
        below.start()

    @pl.when(t >= 1)
    def _():
        above.start()

    advance()

    @pl.when(t >= 1)
    def _():
        below.wait_recv()
        gpad[0:16, :] = hrecv[0].astype(F32)

    @pl.when(t < 1)
    def _():
        gpad[0:16, :] = jnp.zeros((16, half_width), F32)

    @pl.when(t + 1 < n)
    def _():
        above.wait_recv()
        gpad[16 + length : 32 + length, :] = hrecv[1].astype(F32)

    @pl.when(t + 1 >= n)
    def _():
        gpad[16 + length : 32 + length, :] = jnp.zeros((16, half_width), F32)

    finish(3)
    strip = 128

    @pl.loop(0, half_width // 128)
    def _(j):
        cols = pl.ds(pl.multiple_of(j * 128, 128), 128)
        for start in range(0, length, strip):
            conv = jnp.zeros((strip, 128), F32)
            for shift in range(8):
                moved = gpad[start + shift : start + shift + strip + 24, cols]
                for at in range(shift, 32, 8):
                    if at >= 1:
                        conv = conv + taps_ref[at - 1 : at, cols] * moved[at - shift : at - shift + strip]
            pre = conv * scale_ref[:, cols] + shift_ref[:, cols]
            act_s[start : start + strip, cols] = (pre * jax.nn.sigmoid(pre)).astype(BF16)

    ready(3)

    @pl.loop(0, out_ref.shape[1] // TILE)
    def _(j):
        cols = pl.ds(pl.multiple_of(j * TILE, TILE), TILE)
        add = jnp.dot(act_s[...], w_proj[:, cols], preferred_element_type=F32)
        out_ref[:, cols] = (mid_s[:, cols].astype(F32) + add).astype(BF16)

    for w in range(len(pieces)):
        for side, hops in sides:
            for hop in range(hops):
                ring(w, side, hop).wait_send()
                over_x(w, side, hop).wait_send()
        for slot in range(chips):
            over_core(w, slot, t).wait_send()

    @pl.when(t + 1 < n)
    def _():
        near.wait_send()
        near_count.wait_send()
        below.wait_send()

    @pl.when(t >= 1)
    def _():
        above.wait_send()

    @pl.when(t + 2 < n)
    def _():
        far_count.wait_send()

    @pl.when((t + 2 < n) & even)
    def _():
        far.wait_send()

    @pl.when((t >= 1) & even)
    def _():
        relay.wait_send()


def fused(
    n, frames, frame_count, lookback_mask, attn_gain, w_query, w_key, w_value, w_out, conv_gain,
    w_glu, depthwise, conv_scale, conv_shift, w_proj,
):
    length, model = frames.shape
    width = w_query.shape[1]
    half = w_glu.shape[1] // 2
    chips = n // 2
    inside, scalars = (pl.BlockSpec(memory_space=m) for m in (pltpu.VMEM, pltpu.SMEM))
    dma = pltpu.SemaphoreType.DMA
    params = 3 * width * model + model * width + 2 * half * model + half * model
    return pl.pallas_call(
        functools.partial(block, n),
        out_shape=jax.ShapeDtypeStruct((length, model), BF16),
        in_specs=[inside, scalars, scalars] + [inside] * 11,
        out_specs=pl.BlockSpec(memory_space=pltpu.VMEM),
        scratch_shapes=[
            pltpu.VMEM((model, 3 * width), BF16),
            pltpu.VMEM((width, model), BF16),
            pltpu.VMEM((model, 2 * half), BF16),
            pltpu.VMEM((half, model), BF16),
            pltpu.VMEM((3 * length, model), BF16),
            pltpu.VMEM((3, 8, 128), jnp.int32),
            pltpu.VMEM((length, width), BF16),
            pltpu.VMEM((3 * length, 2 * width), BF16),
            pltpu.VMEM((length, width), BF16),
            pltpu.VMEM((length, model), BF16),
            pltpu.VMEM((length, model), BF16),
            pltpu.VMEM((length + 32, half), F32),
            pltpu.VMEM((length, half), BF16),
            pltpu.VMEM((2, 16, half), BF16),
            pltpu.VMEM((2, 16, half), BF16),
            dma((6, chips - 1)), dma((6, chips - 1)),
            dma((6, chips - 1)), dma((6, chips - 1)),
            dma((6, chips)), dma((6, chips)),
            dma((3,)), dma((2,)), dma((2,)), dma((2,)), dma((2,)), dma((2,)),
        ],
        compiler_params=pltpu.CompilerParams(
            collective_id=0, has_side_effects=True, vmem_limit_bytes=56 * 1024 * 1024
        ),
        cost_estimate=pl.CostEstimate(
            flops=2 * length * params, bytes_accessed=2 * params, transcendentals=length * half
        ),
    )(
        frames, frame_count, lookback_mask, attn_gain, w_query, w_key, w_value, w_out,
        conv_gain, w_glu, depthwise, conv_scale.reshape(1, -1),
        conv_shift.reshape(1, -1), w_proj,
    )


def shards(groups, *args):
    n = lax.axis_size("tm")
    frames, w_query, w_out, w_glu, w_proj = args[0], args[4], args[7], args[9], args[13]
    whole = all(w.shape[0] % 16 == 0 and w.shape[0] >= 48 for w in (w_query, w_out, w_glu, w_proj))
    tiles = all(
        w.shape[1] % TILE == 0 for w in (w_query, w_out, w_proj)
    ) and w_glu.shape[1] % (2 * TILE) == 0
    if groups == 2 and n % 8 == 0 and whole and tiles and frames.shape[0] % 256 == 0:
        return fused(n, *args)
    return plain(*args)


def solution(mesh):
    return jax.shard_map(
        functools.partial(shards, mesh.shape["groups"]),
        mesh=mesh,
        in_specs=(
            P(("groups", "tm"), None),
            P(("groups", "tm")),
            P(("groups", "tm"), None),
            P(),
            P("tm", None),
            P("tm", None),
            P("tm", None),
            P("tm", None),
            P(),
            P("tm", None),
            P(),
            P(),
            P(),
            P("tm", None),
        ),
        out_specs=P(("groups", "tm"), None),
        check_vma=False,
    )
```

```python
import functools
import math

import jax
import jax.numpy as jnp
from jax import lax
from jax.experimental import pallas as pl
from jax.experimental.pallas import tpu as pltpu
from jax.sharding import PartitionSpec as P

HEADS = 8
HEAD_DIM = 96
KERNEL = 31


def shifted(block, axis, distance):
    devices = range(lax.axis_size(axis))
    route = [(i - distance, i) for i in devices if i - distance in devices]
    return lax.ppermute(block, axis, route)


def with_halo(value, sides, width):
    for axis, dim in sides:
        size, length = (lax.axis_size(axis), value.shape[dim])
        up = [(i, (i + 1) % size) for i in range(size - 1)]
        down = [(j, i) for i, j in up]
        last = lax.slice_in_dim(value, length - width, length, axis=dim)
        first = lax.slice_in_dim(value, 0, width, axis=dim)
        before = lax.ppermute(last, axis, up)
        after = lax.ppermute(first, axis, down)
        value = jnp.concatenate([before, value, after], axis=dim)
    return value


def normalize(x, gain):
    xf = x.astype(jnp.float32)
    mean = jnp.mean(xf, axis=-1, keepdims=True)
    centered = xf - mean
    var = jnp.mean(centered * centered, axis=-1, keepdims=True)
    return (centered * lax.rsqrt(var + 1e-05) * gain).astype(jnp.bfloat16)


def add_rows(left, piece):
    return jnp.dot(left, piece, preferred_element_type=jnp.float32)


def attend(query_c, keys, values, counts, allowed):
    width = query_c.shape[0]
    pos = jnp.arange(3 * width, dtype=jnp.int32)
    section = pos // width
    place = pos % width
    limit = jnp.where(section == 0, counts[0], jnp.where(section == 1, counts[1], counts[2]))
    block = pos // (width // 2)
    allow = jnp.sum(
        (block[:, None] == jnp.arange(4, dtype=jnp.int32)[None, :]) * allowed[None, :], axis=1
    ) + (block >= 4)
    visible = (place < limit) & (allow > 0)
    factor = 1.0 / math.sqrt(HEAD_DIM)

    def one_head(head):
        start = head * HEAD_DIM
        q_head = lax.dynamic_slice_in_dim(query_c, start, HEAD_DIM, 1)
        k_head = lax.dynamic_slice_in_dim(keys, start, HEAD_DIM, 1)
        v_head = lax.dynamic_slice_in_dim(values, start, HEAD_DIM, 1)
        scores = (
            lax.dot_general(
                q_head, k_head, (((1,), (1,)), ((), ())), preferred_element_type=jnp.float32
            )
            * factor
        )
        scores = jnp.where(visible[None, :], scores, -jnp.inf)
        top = jnp.max(scores, axis=1, keepdims=True)
        expo = jnp.exp(scores - top)
        weights = (expo / jnp.sum(expo, axis=1, keepdims=True)).astype(jnp.bfloat16)
        return jnp.dot(weights, v_head, preferred_element_type=jnp.float32).astype(jnp.bfloat16)

    stacked = lax.map(one_head, jnp.arange(HEADS, dtype=jnp.int32))
    return jnp.transpose(stacked, (1, 0, 2)).reshape(width, HEADS * HEAD_DIM)


def plain(
    frames,
    frame_count,
    lookback_mask,
    attn_gain,
    w_query,
    w_key,
    w_value,
    w_out,
    conv_gain,
    w_glu,
    depthwise,
    conv_scale,
    conv_shift,
    w_proj,
):
    width = frames.shape[0]
    conv_width = w_proj.shape[0] * lax.axis_size("tm")
    norm_a = normalize(frames, attn_gain)
    query = add_rows(norm_a, lax.all_gather(w_query, "tm", axis=0, tiled=True))
    key = add_rows(norm_a, lax.all_gather(w_key, "tm", axis=0, tiled=True))
    value = add_rows(norm_a, lax.all_gather(w_value, "tm", axis=0, tiled=True))
    query = query.astype(jnp.bfloat16)
    key = key.astype(jnp.bfloat16)
    value = value.astype(jnp.bfloat16)
    own = (key, value, frame_count)
    received = []
    current = own
    for step in range(2):
        current = shifted((current[0], current[1], current[2]), "tm", 1)
        received.append(current)
    nearer, farther = (received[0], received[1])
    keys = jnp.concatenate([farther[0], nearer[0], key], axis=0)
    values = jnp.concatenate([farther[1], nearer[1], value], axis=0)
    counts = jnp.concatenate([farther[2], nearer[2], frame_count])
    context = attend(query, keys, values, counts, lookback_mask[0])
    attn_sum = add_rows(context, lax.all_gather(w_out, "tm", axis=0, tiled=True))
    mid = (frames.astype(jnp.float32) + attn_sum).astype(jnp.bfloat16)
    norm_c = normalize(mid, conv_gain)
    glu_in = add_rows(norm_c, lax.all_gather(w_glu, "tm", axis=0, tiled=True))
    live = jnp.arange(width, dtype=jnp.int32) < frame_count[0]
    gated = jnp.where(
        live[:, None], glu_in[:, :conv_width] * jax.nn.sigmoid(glu_in[:, conv_width:]), 0.0
    ).astype(jnp.bfloat16)
    half = KERNEL // 2
    padded = with_halo(gated, (("tm", 0),), half)
    conv = jnp.zeros((width, conv_width), jnp.float32)
    for tap in range(KERNEL):
        conv = conv + depthwise[tap] * padded[tap : tap + width].astype(jnp.float32)
    activated = jax.nn.silu(conv * conv_scale + conv_shift).astype(jnp.bfloat16)
    conv_sum = add_rows(activated, lax.all_gather(w_proj, "tm", axis=0, tiled=True))
    return (mid.astype(jnp.float32) + conv_sum).astype(jnp.bfloat16)


F32 = jnp.float32
BF16 = jnp.bfloat16
MESH = pl.DeviceIdType.MESH
TILE = 256


def norm_rows(source, gain_ref, target):
    rows = source.shape[0]

    @pl.loop(0, rows // 32)
    def _(step):
        at = pl.ds(pl.multiple_of(step * 32, 32), 32)
        xf = source[at, :].astype(F32)
        mean = jnp.mean(xf, axis=-1, keepdims=True)
        centered = xf - mean
        var = jnp.mean(centered * centered, axis=-1, keepdims=True)
        target[at, :] = (centered * lax.rsqrt(var + 1e-05) * gain_ref[...].reshape(1, -1)).astype(BF16)


def block(
    n,
    frames_ref, count_ref, look_ref, gain_a_ref, wq_ref, wk_ref, wv_ref, wo_ref, gain_c_ref,
    wg_ref, taps_ref, scale_ref, shift_ref, wp_ref,
    out_ref,
    w_qkv, w_out, w_glu, w_proj, norm, counts, hide_s, qt_s, k_s, vt_s, ctxt_s, ctx_s, mid_s, normc_s, gpad, act_s,
    hsend, hrecv,
    ring_send, ring_recv, x_send, x_recv, c_send, c_recv, n_send, n_recv, m_send, m_recv,
    h_send, h_recv,
):
    g = lax.axis_index("groups")
    t = lax.axis_index("tm")
    core = lax.rem(t, 2)
    chip = t // 2
    chips = n // 2
    deep = chips // 2
    hops_a, hops_b = chips // 2, chips // 2 - 1
    place = jnp.where(lax.rem(chip, 2) == 0, chip // 2, chips - 1 - chip // 2)
    turn = 1 - 2 * core

    def at_place(r):
        r = lax.rem(r + 2 * chips, chips)
        q = jnp.where(r < deep, 2 * r, 2 * (chips - 1 - r) + 1)
        return 2 * q + core

    next_a, next_b = at_place(place + turn), at_place(place - turn)
    pair = t + turn
    here = lambda index: (g, index)
    across = (1 - g, t)

    weights = (w_qkv, w_out, w_glu, w_proj)
    depth = tuple(w.shape[0] // n for w in weights)
    width = wq_ref.shape[1]
    halves = depth[2] // 2 if depth[2] % 32 == 0 else depth[2]
    pieces = [
        (0, 0, depth[0], width, width, 61),
        (0, 0, depth[0], 2 * width, width, 50),
        (0, 0, depth[0], 0, width, 50),
        (1, 0, depth[1], 0, w_out.shape[1], 61),
        (2, 0, halves, 0, w_glu.shape[1], 61),
        (2, depth[2] - halves, halves, 0, w_glu.shape[1], 61),
        (3, 0, depth[3], 0, w_proj.shape[1], 61),
    ]

    def rows(p, owner, start, size):
        w, low, high, first = pieces[p][:4]
        at = pl.ds(pl.multiple_of(owner * depth[w] + low, 16), high)
        return weights[w].at[at, pl.ds(pl.multiple_of(first + start, 128), size)]

    def sizes(p):
        cols, share = pieces[p][4:]
        return cols, (share * cols + 6400) // 12800 * 128

    def copy(src, dst, send, recv, device):
        return pltpu.make_async_remote_copy(
            src_ref=src, dst_ref=dst, send_sem=send, recv_sem=recv,
            device_id=device, device_id_type=MESH,
        )

    def ring(w, side, hop):
        sign = turn if side == 0 else -turn
        cols, ringed = sizes(w)
        view = rows(w, at_place(place - sign * hop), g * (cols - ringed), ringed)
        slot = hop + side * hops_a
        target = next_a if side == 0 else next_b
        return copy(view, view, ring_send.at[w, slot], ring_recv.at[w, slot], here(target))

    def arrived(side, hop):
        return at_place(place - (turn if side == 0 else -turn) * (hop + 1))

    def over_x(w, side, hop):
        cols, ringed = sizes(w)
        view = rows(w, arrived(side, hop), g * ringed, cols - ringed)
        slot = hop + side * hops_a
        return copy(view, view, x_send.at[w, slot], x_recv.at[w, slot], across)

    def over_core(w, slot, owner):
        view = rows(w, owner, 0, sizes(w)[0])
        return copy(view, view, c_send.at[w, slot], c_recv.at[w, slot], here(pair))

    sides = ((0, hops_a), (1, hops_b))

    def begin(w):
        ring(w, 0, 0).start()
        ring(w, 1, 0).start()
        over_core(w, chips - 1, t).start()

    stepped, spreaded, rounds = set(), set(), []

    def step(w, hop):
        stepped.add((w, hop))
        for side, hops in sides:
            if hop < hops:
                ring(w, side, hop).wait_recv()
                if hop + 1 < hops:
                    ring(w, side, hop + 1).start()
                over_x(w, side, hop).start()

    def spread(w, hop):
        if (w, hop) in spreaded:
            return
        spreaded.add((w, hop))
        for side, hops in sides:
            if hop < hops:
                over_x(w, side, hop).wait_recv()
                over_core(w, hop + side * hops_a, arrived(side, hop)).start()

    turns = (0, 0, 1, 3, 4, 4, 5)

    def advance():
        number = len(rounds)
        rounds.append(number)
        for p, first in enumerate(turns):
            hop = number - first - 1
            if hop == -1:
                begin(p)
            if 0 <= hop < hops_a:
                step(p, hop)
            if 0 < hop <= hops_a:
                spread(p, hop - 1)

    def finish(*which):
        for p in which:
            while (p, hops_a - 1) not in stepped:
                advance()
        for p in which:
            spread(p, hops_a - 1)

    def ready(*which):
        finish(*which)
        for p in which:
            for slot in range(chips):
                over_core(p, slot, t).wait_recv()

    barrier = pltpu.get_barrier_semaphore()
    around = [lax.rem(t + n + d, n) for d in (1, -1, 2, -2)]
    for device in [here(i) for i in (next_a, next_b, pair, *around)] + [across]:
        pl.semaphore_signal(barrier, inc=1, device_id=device, device_id_type=MESH)

    own = lambda w: pl.ds(pl.multiple_of(t * depth[w], 16), depth[w])
    w_qkv[own(0), 0:width] = wq_ref[...]
    w_qkv[own(0), width : 2 * width] = wk_ref[...]
    w_qkv[own(0), 2 * width : 3 * width] = wv_ref[...]
    w_out[own(1), :] = wo_ref[...]
    w_glu[own(2), :] = wg_ref[...]
    w_proj[own(3), :] = wp_ref[...]
    pl.semaphore_wait(barrier, 8)
    advance()

    length = frames_ref.shape[0]
    part = lambda i: norm.at[pl.ds(i * length, length), :]
    norm_rows(frames_ref, gain_a_ref, part(2))
    counts[2] = jnp.full(counts.shape[1:], count_ref[0], jnp.int32)
    near = copy(part(2), part(1), n_send.at[0], n_recv.at[0], here(t + 1))
    far = copy(part(2), part(0), n_send.at[1], n_recv.at[1], here(t + 2))
    relay = copy(part(1), part(0), n_send.at[2], n_recv.at[1], here(t + 1))
    near_count = copy(counts.at[2], counts.at[1], m_send.at[0], m_recv.at[0], here(t + 1))
    far_count = copy(counts.at[2], counts.at[0], m_send.at[1], m_recv.at[1], here(t + 2))
    even = core == 0

    @pl.when(t + 1 < n)
    def _():
        near.start()
        near_count.start()

    @pl.when(t + 2 < n)
    def _():
        far_count.start()

    @pl.when((t + 2 < n) & even)
    def _():
        far.start()

    @pl.when(t < 2)
    def _():
        norm[0:length, :] = jnp.zeros((length, norm.shape[1]), BF16)
        counts[0] = jnp.zeros(counts.shape[1:], jnp.int32)

    @pl.when(t < 1)
    def _():
        norm[length : 2 * length, :] = jnp.zeros((length, norm.shape[1]), BF16)
        counts[1] = jnp.zeros(counts.shape[1:], jnp.int32)

    advance()

    @pl.when(t >= 1)
    def _():
        near.wait_recv()
        near_count.wait_recv()

    @pl.when((t >= 1) & even)
    def _():
        relay.start()

    finish(0)

    @pl.when(t >= 2)
    def _():
        far.wait_recv()
        far_count.wait_recv()

    across_rows = lax.broadcasted_iota(jnp.int32, (128, 128), 0)
    for b in range(3 * length // 128):
        limit = counts[b * 128 // length][0:1, :] - b * 128 % length
        seen = across_rows < limit
        if b * 128 < 2 * length:
            allowed = look_ref[0, b * 128 // (length // 2)]
            seen = seen & (jnp.full((128, 128), allowed, jnp.int32) > 0)
        hide_s[b * 128 : (b + 1) * 128, :] = jnp.where(seen, 0.0, -1e30)

    def tiles(size):
        return lambda body: pl.loop(0, size // TILE)(
            lambda j: body(lambda base: pl.ds(pl.multiple_of(base + j * TILE, TILE), TILE))
        )

    ready(0)

    @tiles(width)
    def _(at):
        k_s[:, at(0)] = jnp.dot(
            norm[...], w_qkv[:, at(width)], preferred_element_type=F32
        ).astype(BF16)

    ready(1)

    @tiles(width)
    def _(at):
        value = jnp.dot(norm[...], w_qkv[:, at(2 * width)], preferred_element_type=F32)
        vt_s[at(0), :] = value.T.astype(BF16)

    ready(2)

    @tiles(width)
    def _(at):
        query = jnp.dot(norm[2 * length :, :], w_qkv[:, at(0)], preferred_element_type=F32)
        qt_s[at(0), :] = query.T.astype(BF16)

    factor = math.log2(math.e) / math.sqrt(HEAD_DIM)
    for head in range(HEADS):
        first = head * HEAD_DIM
        lo = first // 128 * 128
        hi = -(-(first + HEAD_DIM) // 128) * 128
        inside = lax.broadcasted_iota(jnp.int32, (hi - lo, length), 0) + lo
        inside = (inside >= first) & (inside < first + HEAD_DIM)
        q_head = jnp.where(inside, qt_s[lo:hi, :].astype(F32), 0.0).astype(BF16)
        scores = jnp.dot(k_s[:, lo:hi], q_head, preferred_element_type=F32)
        hide = jnp.concatenate([hide_s[...]] * (length // 128), axis=1)
        scores = scores * factor + hide
        top = jnp.max(scores, axis=0, keepdims=True)
        expo = jnp.exp2(scores - top)
        total = jnp.sum(expo, axis=0, keepdims=True)
        context = jnp.dot(
            vt_s[first : first + HEAD_DIM, :], expo.astype(BF16), preferred_element_type=F32
        )
        ctxt_s[first : first + HEAD_DIM, :] = (context / total).astype(BF16)
        if head in (2, 6):
            advance()

    @tiles(width)
    def _(at):
        ctx_s[:, at(0)] = ctxt_s[at(0), :].astype(F32).T.astype(BF16)

    ready(3)

    @pl.loop(0, mid_s.shape[1] // TILE)
    def _(j):
        cols = pl.ds(pl.multiple_of(j * TILE, TILE), TILE)
        add = jnp.dot(ctx_s[...], w_out[:, cols], preferred_element_type=F32)
        mid_s[:, cols] = (frames_ref[:, cols].astype(F32) + add).astype(BF16)

    norm_rows(mid_s, gain_c_ref, normc_s)
    ready(4, 5)

    half_width = w_glu.shape[1] // 2
    live = lax.broadcasted_iota(jnp.int32, (length, 1), 0) < count_ref[0]

    @pl.loop(0, half_width // TILE)
    def _(j):
        cols = pl.ds(pl.multiple_of(j * TILE, TILE), TILE)
        gate_cols = pl.ds(pl.multiple_of(j * TILE + half_width, TILE), TILE)
        left = jnp.dot(normc_s[...], w_glu[:, cols], preferred_element_type=F32)
        gate = jnp.dot(normc_s[...], w_glu[:, gate_cols], preferred_element_type=F32)
        gated = jnp.where(live, left * jax.nn.sigmoid(gate), 0.0).astype(BF16)
        gpad[16 : 16 + length, cols] = gated.astype(F32)
        hsend[0, :, cols] = gated[0:16]
        hsend[1, :, cols] = gated[length - 16 : length]

    below = copy(hsend.at[1], hrecv.at[0], h_send.at[0], h_recv.at[0], here(t + 1))
    above = copy(hsend.at[0], hrecv.at[1], h_send.at[1], h_recv.at[1], here(t - 1))

    @pl.when(t + 1 < n)
    def _():
        below.start()

    @pl.when(t >= 1)
    def _():
        above.start()

    advance()

    @pl.when(t >= 1)
    def _():
        below.wait_recv()
        gpad[0:16, :] = hrecv[0].astype(F32)

    @pl.when(t < 1)
    def _():
        gpad[0:16, :] = jnp.zeros((16, half_width), F32)

    @pl.when(t + 1 < n)
    def _():
        above.wait_recv()
        gpad[16 + length : 32 + length, :] = hrecv[1].astype(F32)

    @pl.when(t + 1 >= n)
    def _():
        gpad[16 + length : 32 + length, :] = jnp.zeros((16, half_width), F32)

    finish(6)
    strip = 128

    @pl.loop(0, half_width // 128)
    def _(j):
        cols = pl.ds(pl.multiple_of(j * 128, 128), 128)
        for start in range(0, length, strip):
            conv = jnp.zeros((strip, 128), F32)
            for shift in range(8):
                moved = gpad[start + shift : start + shift + strip + 24, cols]
                for at in range(shift, 32, 8):
                    if at >= 1:
                        conv = conv + taps_ref[at - 1 : at, cols] * moved[at - shift : at - shift + strip]
            pre = conv * scale_ref[:, cols] + shift_ref[:, cols]
            act_s[start : start + strip, cols] = (pre * jax.nn.sigmoid(pre)).astype(BF16)

    ready(6)

    @pl.loop(0, out_ref.shape[1] // TILE)
    def _(j):
        cols = pl.ds(pl.multiple_of(j * TILE, TILE), TILE)
        add = jnp.dot(act_s[...], w_proj[:, cols], preferred_element_type=F32)
        out_ref[:, cols] = (mid_s[:, cols].astype(F32) + add).astype(BF16)

    for w in range(len(pieces)):
        for side, hops in sides:
            for hop in range(hops):
                ring(w, side, hop).wait_send()
                over_x(w, side, hop).wait_send()
        for slot in range(chips):
            over_core(w, slot, t).wait_send()

    @pl.when(t + 1 < n)
    def _():
        near.wait_send()
        near_count.wait_send()
        below.wait_send()

    @pl.when(t >= 1)
    def _():
        above.wait_send()

    @pl.when(t + 2 < n)
    def _():
        far_count.wait_send()

    @pl.when((t + 2 < n) & even)
    def _():
        far.wait_send()

    @pl.when((t >= 1) & even)
    def _():
        relay.wait_send()


def fused(
    n, frames, frame_count, lookback_mask, attn_gain, w_query, w_key, w_value, w_out, conv_gain,
    w_glu, depthwise, conv_scale, conv_shift, w_proj,
):
    length, model = frames.shape
    width = w_query.shape[1]
    half = w_glu.shape[1] // 2
    chips = n // 2
    inside, scalars = (pl.BlockSpec(memory_space=m) for m in (pltpu.VMEM, pltpu.SMEM))
    dma = pltpu.SemaphoreType.DMA
    params = 3 * width * model + model * width + 2 * half * model + half * model
    return pl.pallas_call(
        functools.partial(block, n),
        out_shape=jax.ShapeDtypeStruct((length, model), BF16),
        in_specs=[inside, scalars, scalars] + [inside] * 11,
        out_specs=pl.BlockSpec(memory_space=pltpu.VMEM),
        scratch_shapes=[
            pltpu.VMEM((model, 3 * width), BF16),
            pltpu.VMEM((width, model), BF16),
            pltpu.VMEM((model, 2 * half), BF16),
            pltpu.VMEM((half, model), BF16),
            pltpu.VMEM((3 * length, model), BF16),
            pltpu.VMEM((3, 8, 128), jnp.int32),
            pltpu.VMEM((3 * length, 128), F32),
            pltpu.VMEM((width, length), BF16),
            pltpu.VMEM((3 * length, width), BF16),
            pltpu.VMEM((width, 3 * length), BF16),
            pltpu.VMEM((width, length), BF16),
            pltpu.VMEM((length, width), BF16),
            pltpu.VMEM((length, model), BF16),
            pltpu.VMEM((length, model), BF16),
            pltpu.VMEM((length + 32, half), F32),
            pltpu.VMEM((length, half), BF16),
            pltpu.VMEM((2, 16, half), BF16),
            pltpu.VMEM((2, 16, half), BF16),
            dma((7, chips - 1)), dma((7, chips - 1)),
            dma((7, chips - 1)), dma((7, chips - 1)),
            dma((7, chips)), dma((7, chips)),
            dma((3,)), dma((2,)), dma((2,)), dma((2,)), dma((2,)), dma((2,)),
        ],
        compiler_params=pltpu.CompilerParams(
            collective_id=0, has_side_effects=True, vmem_limit_bytes=56 * 1024 * 1024
        ),
        cost_estimate=pl.CostEstimate(
            flops=2 * length * params, bytes_accessed=2 * params, transcendentals=length * half
        ),
    )(
        frames, frame_count, lookback_mask, attn_gain, w_query, w_key, w_value, w_out,
        conv_gain, w_glu, depthwise, conv_scale.reshape(1, -1),
        conv_shift.reshape(1, -1), w_proj,
    )


def shards(groups, *args):
    n = lax.axis_size("tm")
    frames, w_query, w_out, w_glu, w_proj = args[0], args[4], args[7], args[9], args[13]
    whole = all(w.shape[0] % 16 == 0 and w.shape[0] >= 48 for w in (w_query, w_out, w_glu, w_proj))
    tiles = all(
        w.shape[1] % TILE == 0 for w in (w_query, w_out, w_proj)
    ) and w_glu.shape[1] % (2 * TILE) == 0
    if groups == 2 and n % 8 == 0 and whole and tiles and frames.shape[0] % 256 == 0:
        return fused(n, *args)
    return plain(*args)


def solution(mesh):
    return jax.shard_map(
        functools.partial(shards, mesh.shape["groups"]),
        mesh=mesh,
        in_specs=(
            P(("groups", "tm"), None),
            P(("groups", "tm")),
            P(("groups", "tm"), None),
            P(),
            P("tm", None),
            P("tm", None),
            P("tm", None),
            P("tm", None),
            P(),
            P("tm", None),
            P(),
            P(),
            P(),
            P("tm", None),
        ),
        out_specs=P(("groups", "tm"), None),
        check_vma=False,
    )
```

```python
import functools
import math

import jax
import jax.numpy as jnp
from jax import lax
from jax.experimental import pallas as pl
from jax.experimental.pallas import tpu as pltpu
from jax.sharding import PartitionSpec as P

HEADS = 8
HEAD_DIM = 96
KERNEL = 31


def shifted(block, axis, distance):
    devices = range(lax.axis_size(axis))
    route = [(i - distance, i) for i in devices if i - distance in devices]
    return lax.ppermute(block, axis, route)


def with_halo(value, sides, width):
    for axis, dim in sides:
        size, length = (lax.axis_size(axis), value.shape[dim])
        up = [(i, (i + 1) % size) for i in range(size - 1)]
        down = [(j, i) for i, j in up]
        last = lax.slice_in_dim(value, length - width, length, axis=dim)
        first = lax.slice_in_dim(value, 0, width, axis=dim)
        before = lax.ppermute(last, axis, up)
        after = lax.ppermute(first, axis, down)
        value = jnp.concatenate([before, value, after], axis=dim)
    return value


def normalize(x, gain):
    xf = x.astype(jnp.float32)
    mean = jnp.mean(xf, axis=-1, keepdims=True)
    centered = xf - mean
    var = jnp.mean(centered * centered, axis=-1, keepdims=True)
    return (centered * lax.rsqrt(var + 1e-05) * gain).astype(jnp.bfloat16)


def add_rows(left, piece):
    return jnp.dot(left, piece, preferred_element_type=jnp.float32)


def attend(query_c, keys, values, counts, allowed):
    width = query_c.shape[0]
    pos = jnp.arange(3 * width, dtype=jnp.int32)
    section = pos // width
    place = pos % width
    limit = jnp.where(section == 0, counts[0], jnp.where(section == 1, counts[1], counts[2]))
    block = pos // (width // 2)
    allow = jnp.sum(
        (block[:, None] == jnp.arange(4, dtype=jnp.int32)[None, :]) * allowed[None, :], axis=1
    ) + (block >= 4)
    visible = (place < limit) & (allow > 0)
    factor = 1.0 / math.sqrt(HEAD_DIM)

    def one_head(head):
        start = head * HEAD_DIM
        q_head = lax.dynamic_slice_in_dim(query_c, start, HEAD_DIM, 1)
        k_head = lax.dynamic_slice_in_dim(keys, start, HEAD_DIM, 1)
        v_head = lax.dynamic_slice_in_dim(values, start, HEAD_DIM, 1)
        scores = (
            lax.dot_general(
                q_head, k_head, (((1,), (1,)), ((), ())), preferred_element_type=jnp.float32
            )
            * factor
        )
        scores = jnp.where(visible[None, :], scores, -jnp.inf)
        top = jnp.max(scores, axis=1, keepdims=True)
        expo = jnp.exp(scores - top)
        weights = (expo / jnp.sum(expo, axis=1, keepdims=True)).astype(jnp.bfloat16)
        return jnp.dot(weights, v_head, preferred_element_type=jnp.float32).astype(jnp.bfloat16)

    stacked = lax.map(one_head, jnp.arange(HEADS, dtype=jnp.int32))
    return jnp.transpose(stacked, (1, 0, 2)).reshape(width, HEADS * HEAD_DIM)


def plain(
    frames,
    frame_count,
    lookback_mask,
    attn_gain,
    w_query,
    w_key,
    w_value,
    w_out,
    conv_gain,
    w_glu,
    depthwise,
    conv_scale,
    conv_shift,
    w_proj,
):
    width = frames.shape[0]
    conv_width = w_proj.shape[0] * lax.axis_size("tm")
    norm_a = normalize(frames, attn_gain)
    query = add_rows(norm_a, lax.all_gather(w_query, "tm", axis=0, tiled=True))
    key = add_rows(norm_a, lax.all_gather(w_key, "tm", axis=0, tiled=True))
    value = add_rows(norm_a, lax.all_gather(w_value, "tm", axis=0, tiled=True))
    query = query.astype(jnp.bfloat16)
    key = key.astype(jnp.bfloat16)
    value = value.astype(jnp.bfloat16)
    own = (key, value, frame_count)
    received = []
    current = own
    for step in range(2):
        current = shifted((current[0], current[1], current[2]), "tm", 1)
        received.append(current)
    nearer, farther = (received[0], received[1])
    keys = jnp.concatenate([farther[0], nearer[0], key], axis=0)
    values = jnp.concatenate([farther[1], nearer[1], value], axis=0)
    counts = jnp.concatenate([farther[2], nearer[2], frame_count])
    context = attend(query, keys, values, counts, lookback_mask[0])
    attn_sum = add_rows(context, lax.all_gather(w_out, "tm", axis=0, tiled=True))
    mid = (frames.astype(jnp.float32) + attn_sum).astype(jnp.bfloat16)
    norm_c = normalize(mid, conv_gain)
    glu_in = add_rows(norm_c, lax.all_gather(w_glu, "tm", axis=0, tiled=True))
    live = jnp.arange(width, dtype=jnp.int32) < frame_count[0]
    gated = jnp.where(
        live[:, None], glu_in[:, :conv_width] * jax.nn.sigmoid(glu_in[:, conv_width:]), 0.0
    ).astype(jnp.bfloat16)
    half = KERNEL // 2
    padded = with_halo(gated, (("tm", 0),), half)
    conv = jnp.zeros((width, conv_width), jnp.float32)
    for tap in range(KERNEL):
        conv = conv + depthwise[tap] * padded[tap : tap + width].astype(jnp.float32)
    activated = jax.nn.silu(conv * conv_scale + conv_shift).astype(jnp.bfloat16)
    conv_sum = add_rows(activated, lax.all_gather(w_proj, "tm", axis=0, tiled=True))
    return (mid.astype(jnp.float32) + conv_sum).astype(jnp.bfloat16)


F32 = jnp.float32
BF16 = jnp.bfloat16
MESH = pl.DeviceIdType.MESH
TILE = 256


def norm_rows(source, gain_ref, target):
    rows = source.shape[0]

    @pl.loop(0, rows // 32)
    def _(step):
        at = pl.ds(pl.multiple_of(step * 32, 32), 32)
        xf = source[at, :].astype(F32)
        mean = jnp.mean(xf, axis=-1, keepdims=True)
        centered = xf - mean
        var = jnp.mean(centered * centered, axis=-1, keepdims=True)
        target[at, :] = (centered * lax.rsqrt(var + 1e-05) * gain_ref[...].reshape(1, -1)).astype(BF16)


def block(
    n,
    frames_ref, count_ref, look_ref, gain_a_ref, wq_ref, wk_ref, wv_ref, wo_ref, gain_c_ref,
    wg_ref, taps_ref, scale_ref, shift_ref, wp_ref,
    out_ref,
    w_qkv, w_out, w_glu, w_proj, norm, counts, q_s, kv_s, ctx_s, mid_s, normc_s, gpad, act_s,
    hsend, hrecv,
    ring_send, ring_recv, x_send, x_recv, c_send, c_recv, n_send, n_recv, m_send, m_recv,
    h_send, h_recv,
):
    g = lax.axis_index("groups")
    t = lax.axis_index("tm")
    core = lax.rem(t, 2)
    chip = t // 2
    chips = n // 2
    deep = chips // 2
    hops_a, hops_b = chips // 2, chips // 2 - 1
    place = jnp.where(lax.rem(chip, 2) == 0, chip // 2, chips - 1 - chip // 2)
    turn = 1 - 2 * core

    def at_place(r):
        r = lax.rem(r + 2 * chips, chips)
        q = jnp.where(r < deep, 2 * r, 2 * (chips - 1 - r) + 1)
        return 2 * q + core

    next_a, next_b = at_place(place + turn), at_place(place - turn)
    pair = t + turn
    here = lambda index: (g, index)
    across = (1 - g, t)

    weights = (w_qkv, w_out, w_glu, w_proj)
    depth = tuple(w.shape[0] // n for w in weights)
    width = wq_ref.shape[1]
    part_q, part_g = width // 2, w_glu.shape[1] // 4
    pieces = (
        (0, 0, 3 * part_q, 55),
        (0, 3 * part_q, 3 * part_q, 55),
        (1, 0, w_out.shape[1], 61),
        (2, 0, 2 * part_g, 61),
        (2, 2 * part_g, 2 * part_g, 61),
        (3, 0, w_proj.shape[1], 61),
    )

    def rows(p, owner, start, size):
        w, first = pieces[p][:2]
        at = pl.ds(pl.multiple_of(owner * depth[w], 16), depth[w])
        return weights[w].at[at, pl.ds(pl.multiple_of(first + start, 128), size)]

    def sizes(p):
        cols, share = pieces[p][2:]
        return cols, (share * cols + 6400) // 12800 * 128

    def copy(src, dst, send, recv, device):
        return pltpu.make_async_remote_copy(
            src_ref=src, dst_ref=dst, send_sem=send, recv_sem=recv,
            device_id=device, device_id_type=MESH,
        )

    def ring(w, side, hop):
        sign = turn if side == 0 else -turn
        cols, ringed = sizes(w)
        view = rows(w, at_place(place - sign * hop), g * (cols - ringed), ringed)
        slot = hop + side * hops_a
        target = next_a if side == 0 else next_b
        return copy(view, view, ring_send.at[w, slot], ring_recv.at[w, slot], here(target))

    def arrived(side, hop):
        return at_place(place - (turn if side == 0 else -turn) * (hop + 1))

    def over_x(w, side, hop):
        cols, ringed = sizes(w)
        view = rows(w, arrived(side, hop), g * ringed, cols - ringed)
        slot = hop + side * hops_a
        return copy(view, view, x_send.at[w, slot], x_recv.at[w, slot], across)

    def over_core(w, slot, owner):
        view = rows(w, owner, 0, sizes(w)[0])
        return copy(view, view, c_send.at[w, slot], c_recv.at[w, slot], here(pair))

    sides = ((0, hops_a), (1, hops_b))

    def begin(w):
        ring(w, 0, 0).start()
        ring(w, 1, 0).start()
        over_core(w, chips - 1, t).start()

    stepped, spreaded, rounds = set(), set(), []

    def step(w, hop):
        stepped.add((w, hop))
        for side, hops in sides:
            if hop < hops:
                ring(w, side, hop).wait_recv()
                if hop + 1 < hops:
                    ring(w, side, hop + 1).start()
                over_x(w, side, hop).start()

    def spread(w, hop):
        if (w, hop) in spreaded:
            return
        spreaded.add((w, hop))
        for side, hops in sides:
            if hop < hops:
                over_x(w, side, hop).wait_recv()
                over_core(w, hop + side * hops_a, arrived(side, hop)).start()

    turns = (0, 1, 3, 4, 5, 6)

    def advance():
        number = len(rounds)
        rounds.append(number)
        for p, first in enumerate(turns):
            hop = number - first - 1
            if hop == -1:
                begin(p)
            if 0 <= hop < hops_a:
                step(p, hop)
            if 0 < hop <= hops_a:
                spread(p, hop - 1)

    def finish(p):
        while (p, hops_a - 1) not in stepped:
            advance()
        spread(p, hops_a - 1)

    def ready(p):
        finish(p)
        for slot in range(chips):
            over_core(p, slot, t).wait_recv()

    barrier = pltpu.get_barrier_semaphore()
    around = [lax.rem(t + n + d, n) for d in (1, -1, 2, -2)]
    for device in [here(i) for i in (next_a, next_b, pair, *around)] + [across]:
        pl.semaphore_signal(barrier, inc=1, device_id=device, device_id_type=MESH)

    own = lambda w: pl.ds(pl.multiple_of(t * depth[w], 16), depth[w])
    for half in range(2):
        for i, ref in enumerate((wk_ref, wv_ref, wq_ref)):
            first = (3 * half + i) * part_q
            w_qkv[own(0), first : first + part_q] = ref[:, half * part_q : (half + 1) * part_q]
        for i in range(2):
            first = (2 * half + i) * part_g
            there = (2 * i + half) * part_g
            w_glu[own(2), first : first + part_g] = wg_ref[:, there : there + part_g]
    w_out[own(1), :] = wo_ref[...]
    w_proj[own(3), :] = wp_ref[...]
    pl.semaphore_wait(barrier, 8)
    advance()

    length = frames_ref.shape[0]
    part = lambda i: norm.at[pl.ds(i * length, length), :]
    norm_rows(frames_ref, gain_a_ref, part(2))
    counts[2] = jnp.full(counts.shape[1:], count_ref[0], jnp.int32)
    near = copy(part(2), part(1), n_send.at[0], n_recv.at[0], here(t + 1))
    far = copy(part(2), part(0), n_send.at[1], n_recv.at[1], here(t + 2))
    relay = copy(part(1), part(0), n_send.at[2], n_recv.at[1], here(t + 1))
    near_count = copy(counts.at[2], counts.at[1], m_send.at[0], m_recv.at[0], here(t + 1))
    far_count = copy(counts.at[2], counts.at[0], m_send.at[1], m_recv.at[1], here(t + 2))
    even = core == 0

    @pl.when(t + 1 < n)
    def _():
        near.start()
        near_count.start()

    @pl.when(t + 2 < n)
    def _():
        far_count.start()

    @pl.when((t + 2 < n) & even)
    def _():
        far.start()

    @pl.when(t < 2)
    def _():
        norm[0:length, :] = jnp.zeros((length, norm.shape[1]), BF16)
        counts[0] = jnp.zeros(counts.shape[1:], jnp.int32)

    @pl.when(t < 1)
    def _():
        norm[length : 2 * length, :] = jnp.zeros((length, norm.shape[1]), BF16)
        counts[1] = jnp.zeros(counts.shape[1:], jnp.int32)

    ctx_s[...] = jnp.zeros_like(ctx_s)

    advance()

    @pl.when(t >= 1)
    def _():
        near.wait_recv()
        near_count.wait_recv()

    @pl.when((t >= 1) & even)
    def _():
        relay.start()

    finish(0)

    @pl.when(t >= 2)
    def _():
        far.wait_recv()
        far_count.wait_recv()

    lane = lax.broadcasted_iota(jnp.int32, (1, 128), 1)
    hide = []
    for b in range(3 * length // 128):
        limit = counts[b * 128 // length][0:1, :] - b * 128 % length
        seen = lane < limit
        if b * 128 < 2 * length:
            seen = seen & (jnp.full((1, 128), look_ref[0, b * 128 // (length // 2)], jnp.int32) > 0)
        hide.append(jnp.where(seen, 0.0, -1e30))
    hide = jnp.concatenate(hide, axis=1)
    factor = math.log2(math.e) / math.sqrt(HEAD_DIM)

    def project(half):
        base = 3 * half * part_q

        @pl.loop(0, 2 * part_q // TILE)
        def _(j):
            cols = pl.ds(pl.multiple_of(2 * half * part_q + j * TILE, TILE), TILE)
            source = pl.ds(pl.multiple_of(base + j * TILE, 128), TILE)
            kv_s[:, cols] = jnp.dot(
                norm[...], w_qkv[:, source], preferred_element_type=F32
            ).astype(BF16)

        q_s[:, half * part_q : (half + 1) * part_q] = jnp.dot(
            norm[2 * length :, :],
            w_qkv[:, base + 2 * part_q : base + 3 * part_q],
            preferred_element_type=F32,
        ).astype(BF16)

    def attend_head(head):
        half, first = head // (HEADS // 2), head % (HEADS // 2) * HEAD_DIM
        lo = first // 128 * 128
        hi = -(-(first + HEAD_DIM) // 128) * 128
        inside = lax.broadcasted_iota(jnp.int32, (length, hi - lo), 1) + lo
        inside = (inside >= first) & (inside < first + HEAD_DIM)
        q_at = slice(half * part_q + lo, half * part_q + hi)
        k_at = slice(2 * half * part_q + lo, 2 * half * part_q + hi)
        v_at = slice((2 * half + 1) * part_q + lo, (2 * half + 1) * part_q + hi)
        q_head = jnp.where(inside, q_s[:, q_at].astype(F32), 0.0).astype(BF16)
        scores = lax.dot_general(
            q_head, kv_s[:, k_at], (((1,), (1,)), ((), ())), preferred_element_type=F32
        )
        scores = scores * factor + hide
        top = jnp.max(scores, axis=1, keepdims=True)
        expo = jnp.exp2(scores - top)
        total = jnp.sum(expo, axis=1, keepdims=True)
        context = jnp.dot(expo.astype(BF16), kv_s[:, v_at], preferred_element_type=F32)
        context = context / total
        ctx_s[:, q_at] = jnp.where(inside, context, ctx_s[:, q_at].astype(F32)).astype(BF16)

    heads = HEADS // 2
    ready(0)
    project(0)
    advance()
    for head in range(heads):
        attend_head(head)
        if head == 1:
            advance()
    ready(1)
    project(1)
    advance()
    for head in range(heads, HEADS):
        attend_head(head)
        if head == heads + 1:
            advance()
    ready(2)

    @pl.loop(0, mid_s.shape[1] // TILE)
    def _(j):
        cols = pl.ds(pl.multiple_of(j * TILE, TILE), TILE)
        add = jnp.dot(ctx_s[...], w_out[:, cols], preferred_element_type=F32)
        mid_s[:, cols] = (frames_ref[:, cols].astype(F32) + add).astype(BF16)

    norm_rows(mid_s, gain_c_ref, normc_s)
    ready(3)

    half_width = 2 * part_g
    live = lax.broadcasted_iota(jnp.int32, (length, 1), 0) < count_ref[0]

    def gate(half):
        @pl.loop(0, part_g // TILE)
        def _(j):
            cols = pl.ds(pl.multiple_of(half * part_g + j * TILE, TILE), TILE)
            left_cols = pl.ds(pl.multiple_of(2 * half * part_g + j * TILE, TILE), TILE)
            gate_cols = pl.ds(pl.multiple_of((2 * half + 1) * part_g + j * TILE, TILE), TILE)
            left = jnp.dot(normc_s[...], w_glu[:, left_cols], preferred_element_type=F32)
            right = jnp.dot(normc_s[...], w_glu[:, gate_cols], preferred_element_type=F32)
            gated = jnp.where(live, left * jax.nn.sigmoid(right), 0.0).astype(BF16)
            gpad[16 : 16 + length, cols] = gated.astype(F32)
            hsend[0, :, cols] = gated[0:16]
            hsend[1, :, cols] = gated[length - 16 : length]

    def halo(half, side):
        cols = pl.ds(half * part_g, part_g)
        return copy(
            hsend.at[1 - side, :, cols], hrecv.at[side, :, cols],
            h_send.at[half, side], h_recv.at[half, side], here(t + 1 - 2 * side),
        )

    def send_halo(half):

        @pl.when(t + 1 < n)
        def _():
            halo(half, 0).start()

        @pl.when(t >= 1)
        def _():
            halo(half, 1).start()

    strip = 128

    def convolve(half):
        cols = pl.ds(half * part_g, part_g)

        @pl.when(t >= 1)
        def _():
            halo(half, 0).wait_recv()
            gpad[0:16, cols] = hrecv[0, :, cols].astype(F32)

        @pl.when(t < 1)
        def _():
            gpad[0:16, cols] = jnp.zeros((16, part_g), F32)

        @pl.when(t + 1 < n)
        def _():
            halo(half, 1).wait_recv()
            gpad[16 + length : 32 + length, cols] = hrecv[1, :, cols].astype(F32)

        @pl.when(t + 1 >= n)
        def _():
            gpad[16 + length : 32 + length, cols] = jnp.zeros((16, part_g), F32)

        @pl.loop(0, part_g // 128)
        def _(j):
            cols = pl.ds(pl.multiple_of(half * part_g + j * 128, 128), 128)
            for start in range(0, length, strip):
                conv = jnp.zeros((strip, 128), F32)
                for shift in range(8):
                    moved = gpad[start + shift : start + shift + strip + 24, cols]
                    for at in range(shift, 32, 8):
                        if at >= 1:
                            conv = conv + taps_ref[at - 1 : at, cols] * moved[at - shift : at - shift + strip]
                pre = conv * scale_ref[:, cols] + shift_ref[:, cols]
                act_s[start : start + strip, cols] = (pre * jax.nn.sigmoid(pre)).astype(BF16)

    gate(0)
    send_halo(0)
    finish(4)
    convolve(0)
    ready(4)
    gate(1)
    send_halo(1)
    finish(5)
    convolve(1)
    ready(5)

    @pl.loop(0, out_ref.shape[1] // TILE)
    def _(j):
        cols = pl.ds(pl.multiple_of(j * TILE, TILE), TILE)
        add = jnp.dot(act_s[...], w_proj[:, cols], preferred_element_type=F32)
        out_ref[:, cols] = (mid_s[:, cols].astype(F32) + add).astype(BF16)

    for w in range(len(pieces)):
        for side, hops in sides:
            for hop in range(hops):
                ring(w, side, hop).wait_send()
                over_x(w, side, hop).wait_send()
        for slot in range(chips):
            over_core(w, slot, t).wait_send()

    @pl.when(t + 1 < n)
    def _():
        near.wait_send()
        near_count.wait_send()
        for half in range(2):
            halo(half, 0).wait_send()

    @pl.when(t >= 1)
    def _():
        for half in range(2):
            halo(half, 1).wait_send()

    @pl.when(t + 2 < n)
    def _():
        far_count.wait_send()

    @pl.when((t + 2 < n) & even)
    def _():
        far.wait_send()

    @pl.when((t >= 1) & even)
    def _():
        relay.wait_send()


def fused(
    n, frames, frame_count, lookback_mask, attn_gain, w_query, w_key, w_value, w_out, conv_gain,
    w_glu, depthwise, conv_scale, conv_shift, w_proj,
):
    length, model = frames.shape
    width = w_query.shape[1]
    half = w_glu.shape[1] // 2
    chips = n // 2
    inside, scalars = (pl.BlockSpec(memory_space=m) for m in (pltpu.VMEM, pltpu.SMEM))
    dma = pltpu.SemaphoreType.DMA
    params = 3 * width * model + model * width + 2 * half * model + half * model
    return pl.pallas_call(
        functools.partial(block, n),
        out_shape=jax.ShapeDtypeStruct((length, model), BF16),
        in_specs=[inside, scalars, scalars] + [inside] * 11,
        out_specs=pl.BlockSpec(memory_space=pltpu.VMEM),
        scratch_shapes=[
            pltpu.VMEM((model, 3 * width), BF16),
            pltpu.VMEM((width, model), BF16),
            pltpu.VMEM((model, 2 * half), BF16),
            pltpu.VMEM((half, model), BF16),
            pltpu.VMEM((3 * length, model), BF16),
            pltpu.VMEM((3, 8, 128), jnp.int32),
            pltpu.VMEM((length, width), BF16),
            pltpu.VMEM((3 * length, 2 * width), BF16),
            pltpu.VMEM((length, width), BF16),
            pltpu.VMEM((length, model), BF16),
            pltpu.VMEM((length, model), BF16),
            pltpu.VMEM((length + 32, half), F32),
            pltpu.VMEM((length, half), BF16),
            pltpu.VMEM((2, 16, half), BF16),
            pltpu.VMEM((2, 16, half), BF16),
            dma((6, chips - 1)), dma((6, chips - 1)),
            dma((6, chips - 1)), dma((6, chips - 1)),
            dma((6, chips)), dma((6, chips)),
            dma((3,)), dma((2,)), dma((2,)), dma((2,)), dma((2, 2)), dma((2, 2)),
        ],
        compiler_params=pltpu.CompilerParams(
            collective_id=0, has_side_effects=True, vmem_limit_bytes=56 * 1024 * 1024
        ),
        cost_estimate=pl.CostEstimate(
            flops=2 * length * params, bytes_accessed=2 * params, transcendentals=length * half
        ),
    )(
        frames, frame_count, lookback_mask, attn_gain, w_query, w_key, w_value, w_out,
        conv_gain, w_glu, depthwise, conv_scale.reshape(1, -1),
        conv_shift.reshape(1, -1), w_proj,
    )


def shards(groups, *args):
    n = lax.axis_size("tm")
    frames, w_query, w_out, w_glu, w_proj = args[0], args[4], args[7], args[9], args[13]
    whole = all(w.shape[0] % 16 == 0 and w.shape[0] >= 48 for w in (w_query, w_out, w_glu, w_proj))
    tiles = all(
        w.shape[1] % TILE == 0 for w in (w_query, w_out, w_proj)
    ) and w_glu.shape[1] % (4 * TILE) == 0
    if groups == 2 and n % 8 == 0 and whole and tiles and frames.shape[0] % 256 == 0:
        return fused(n, *args)
    return plain(*args)


def solution(mesh):
    return jax.shard_map(
        functools.partial(shards, mesh.shape["groups"]),
        mesh=mesh,
        in_specs=(
            P(("groups", "tm"), None),
            P(("groups", "tm")),
            P(("groups", "tm"), None),
            P(),
            P("tm", None),
            P("tm", None),
            P("tm", None),
            P("tm", None),
            P(),
            P("tm", None),
            P(),
            P(),
            P(),
            P("tm", None),
        ),
        out_specs=P(("groups", "tm"), None),
        check_vma=False,
    )
```

```python
import functools
import math

import jax
import jax.numpy as jnp
from jax import lax
from jax.experimental import pallas as pl
from jax.experimental.pallas import tpu as pltpu
from jax.sharding import PartitionSpec as P

HEADS = 8
HEAD_DIM = 96
KERNEL = 31


def shifted(block, axis, distance):
    devices = range(lax.axis_size(axis))
    route = [(i - distance, i) for i in devices if i - distance in devices]
    return lax.ppermute(block, axis, route)


def with_halo(value, sides, width):
    for axis, dim in sides:
        size, length = (lax.axis_size(axis), value.shape[dim])
        up = [(i, (i + 1) % size) for i in range(size - 1)]
        down = [(j, i) for i, j in up]
        last = lax.slice_in_dim(value, length - width, length, axis=dim)
        first = lax.slice_in_dim(value, 0, width, axis=dim)
        before = lax.ppermute(last, axis, up)
        after = lax.ppermute(first, axis, down)
        value = jnp.concatenate([before, value, after], axis=dim)
    return value


def normalize(x, gain):
    xf = x.astype(jnp.float32)
    mean = jnp.mean(xf, axis=-1, keepdims=True)
    centered = xf - mean
    var = jnp.mean(centered * centered, axis=-1, keepdims=True)
    return (centered * lax.rsqrt(var + 1e-05) * gain).astype(jnp.bfloat16)


def add_rows(left, piece):
    return jnp.dot(left, piece, preferred_element_type=jnp.float32)


def attend(query_c, keys, values, counts, allowed):
    width = query_c.shape[0]
    pos = jnp.arange(3 * width, dtype=jnp.int32)
    section = pos // width
    place = pos % width
    limit = jnp.where(section == 0, counts[0], jnp.where(section == 1, counts[1], counts[2]))
    block = pos // (width // 2)
    allow = jnp.sum(
        (block[:, None] == jnp.arange(4, dtype=jnp.int32)[None, :]) * allowed[None, :], axis=1
    ) + (block >= 4)
    visible = (place < limit) & (allow > 0)
    factor = 1.0 / math.sqrt(HEAD_DIM)

    def one_head(head):
        start = head * HEAD_DIM
        q_head = lax.dynamic_slice_in_dim(query_c, start, HEAD_DIM, 1)
        k_head = lax.dynamic_slice_in_dim(keys, start, HEAD_DIM, 1)
        v_head = lax.dynamic_slice_in_dim(values, start, HEAD_DIM, 1)
        scores = (
            lax.dot_general(
                q_head, k_head, (((1,), (1,)), ((), ())), preferred_element_type=jnp.float32
            )
            * factor
        )
        scores = jnp.where(visible[None, :], scores, -jnp.inf)
        top = jnp.max(scores, axis=1, keepdims=True)
        expo = jnp.exp(scores - top)
        weights = (expo / jnp.sum(expo, axis=1, keepdims=True)).astype(jnp.bfloat16)
        return jnp.dot(weights, v_head, preferred_element_type=jnp.float32).astype(jnp.bfloat16)

    stacked = lax.map(one_head, jnp.arange(HEADS, dtype=jnp.int32))
    return jnp.transpose(stacked, (1, 0, 2)).reshape(width, HEADS * HEAD_DIM)


def plain(
    frames,
    frame_count,
    lookback_mask,
    attn_gain,
    w_query,
    w_key,
    w_value,
    w_out,
    conv_gain,
    w_glu,
    depthwise,
    conv_scale,
    conv_shift,
    w_proj,
):
    width = frames.shape[0]
    conv_width = w_proj.shape[0] * lax.axis_size("tm")
    norm_a = normalize(frames, attn_gain)
    query = add_rows(norm_a, lax.all_gather(w_query, "tm", axis=0, tiled=True))
    key = add_rows(norm_a, lax.all_gather(w_key, "tm", axis=0, tiled=True))
    value = add_rows(norm_a, lax.all_gather(w_value, "tm", axis=0, tiled=True))
    query = query.astype(jnp.bfloat16)
    key = key.astype(jnp.bfloat16)
    value = value.astype(jnp.bfloat16)
    own = (key, value, frame_count)
    received = []
    current = own
    for step in range(2):
        current = shifted((current[0], current[1], current[2]), "tm", 1)
        received.append(current)
    nearer, farther = (received[0], received[1])
    keys = jnp.concatenate([farther[0], nearer[0], key], axis=0)
    values = jnp.concatenate([farther[1], nearer[1], value], axis=0)
    counts = jnp.concatenate([farther[2], nearer[2], frame_count])
    context = attend(query, keys, values, counts, lookback_mask[0])
    attn_sum = add_rows(context, lax.all_gather(w_out, "tm", axis=0, tiled=True))
    mid = (frames.astype(jnp.float32) + attn_sum).astype(jnp.bfloat16)
    norm_c = normalize(mid, conv_gain)
    glu_in = add_rows(norm_c, lax.all_gather(w_glu, "tm", axis=0, tiled=True))
    live = jnp.arange(width, dtype=jnp.int32) < frame_count[0]
    gated = jnp.where(
        live[:, None], glu_in[:, :conv_width] * jax.nn.sigmoid(glu_in[:, conv_width:]), 0.0
    ).astype(jnp.bfloat16)
    half = KERNEL // 2
    padded = with_halo(gated, (("tm", 0),), half)
    conv = jnp.zeros((width, conv_width), jnp.float32)
    for tap in range(KERNEL):
        conv = conv + depthwise[tap] * padded[tap : tap + width].astype(jnp.float32)
    activated = jax.nn.silu(conv * conv_scale + conv_shift).astype(jnp.bfloat16)
    conv_sum = add_rows(activated, lax.all_gather(w_proj, "tm", axis=0, tiled=True))
    return (mid.astype(jnp.float32) + conv_sum).astype(jnp.bfloat16)


F32 = jnp.float32
BF16 = jnp.bfloat16
MESH = pl.DeviceIdType.MESH
TILE = 256


def norm_rows(source, gain_ref, target):
    rows = source.shape[0]

    @pl.loop(0, rows // 32)
    def _(step):
        at = pl.ds(pl.multiple_of(step * 32, 32), 32)
        xf = source[at, :].astype(F32)
        mean = jnp.mean(xf, axis=-1, keepdims=True)
        centered = xf - mean
        var = jnp.mean(centered * centered, axis=-1, keepdims=True)
        target[at, :] = (centered * lax.rsqrt(var + 1e-05) * gain_ref[...].reshape(1, -1)).astype(BF16)


def block(
    n,
    frames_ref, count_ref, look_ref, gain_a_ref, wq_ref, wk_ref, wv_ref, wo_ref, gain_c_ref,
    wg_ref, taps_ref, scale_ref, shift_ref, wp_ref,
    out_ref,
    w_qkv, w_out, w_glu, w_proj, g_qkv, g_out, g_glu, g_proj, g_frames, res, norm, meta,
    q_s, kv_s, ctx_s, mid_s, normc_s, gpad, act_s, hsend, hrecv, osend, orecv,
    ring_send, ring_recv, x_send, x_recv, c_send, c_recv, n_send, n_recv, m_send, m_recv,
    h_send, h_recv, e_send, e_recv,
):
    g = lax.axis_index("groups")
    t = lax.axis_index("tm")
    core = lax.rem(t, 2)
    other = 1 - core
    chip = t // 2
    chips = n // 2
    deep = chips // 2
    hops_a, hops_b = chips // 2, chips // 2 - 1
    place = jnp.where(lax.rem(chip, 2) == 0, chip // 2, chips - 1 - chip // 2)
    turn = 1 - 2 * core

    def at_place(r):
        r = lax.rem(r + 2 * chips, chips)
        return jnp.where(r < deep, 2 * r, 2 * (chips - 1 - r) + 1)

    here = lambda index: (g, index)
    next_a = here(2 * at_place(place + turn) + core)
    next_b = here(2 * at_place(place - turn) + core)
    pair = here(t + turn)
    across = (1 - g, t)

    weights = (w_qkv, w_out, w_glu, w_proj)
    depth = tuple(w.shape[0] // n for w in weights)
    length, model = frames_ref.shape
    part_q, part_d, part_g = wq_ref.shape[1] // 2, model // 2, wg_ref.shape[1] // 4
    pieces = (
        (0, 0, 2 * part_q, 50),
        (0, 2 * part_q, part_q, 66),
        (1, 0, part_d, 66),
        (2, 0, part_g, 50),
        (2, part_g, part_g, 75),
        (3, 0, part_d, 66),
    )
    turns = (0, 0, 2, 3, 3, 4)

    def rows(p, owner, start, size):
        w, first = pieces[p][:2]
        at = pl.ds(pl.multiple_of(owner * 2 * depth[w], 16), 2 * depth[w])
        return weights[w].at[at, pl.ds(pl.multiple_of(first + start, 128), size)]

    def sizes(p):
        cols, share = pieces[p][2:]
        return cols, (share * cols + 6400) // 12800 * 128

    def copy(src, dst, send, recv, device):
        return pltpu.make_async_remote_copy(
            src_ref=src, dst_ref=dst, send_sem=send, recv_sem=recv,
            device_id=device, device_id_type=MESH,
        )

    def ring(p, side, hop):
        sign = turn if side == 0 else -turn
        cols, ringed = sizes(p)
        view = rows(p, at_place(place - sign * hop), g * (cols - ringed), ringed)
        slot = hop + side * hops_a
        target = next_a if side == 0 else next_b
        return copy(view, view, ring_send.at[p, slot], ring_recv.at[p, slot], target)

    def over_x(p, side, hop):
        owner = at_place(place - (turn if side == 0 else -turn) * (hop + 1))
        cols, ringed = sizes(p)
        view = rows(p, owner, g * ringed, cols - ringed)
        slot = hop + side * hops_a
        return copy(view, view, x_send.at[p, slot], x_recv.at[p, slot], across)

    sides = ((0, hops_a), (1, hops_b))
    own = lambda w: pl.ds(pl.multiple_of(t * depth[w], 16), depth[w])
    given = (g_qkv, g_out, g_glu, g_proj)

    def give(w):
        return copy(given[w], weights[w].at[own(w), :], c_send.at[w], c_recv.at[w], pair)

    got, stepped, rounds = set(), set(), []

    def begin(p):
        w = pieces[p][0]
        if w not in got:
            got.add(w)
            give(w).wait_recv()
        ring(p, 0, 0).start()
        ring(p, 1, 0).start()

    def step(p, hop):
        stepped.add((p, hop))
        for side, hops in sides:
            if hop < hops:
                ring(p, side, hop).wait_recv()
                if hop + 1 < hops:
                    ring(p, side, hop + 1).start()
                over_x(p, side, hop).start()

    def advance():
        number = len(rounds)
        rounds.append(number)
        for p, first in enumerate(turns):
            hop = number - first - 1
            if hop == -1:
                begin(p)
            if 0 <= hop < hops_a:
                step(p, hop)

    def ready(*which):
        for p in which:
            while (p, hops_a - 1) not in stepped:
                advance()
        for p in which:
            for side, hops in sides:
                for hop in range(hops):
                    over_x(p, side, hop).wait_recv()

    barrier = pltpu.get_barrier_semaphore()
    around = [here(lax.rem(t + n + d, n)) for d in (2, -2)]
    for device in [next_a, next_b, pair, across] + around:
        pl.semaphore_signal(barrier, inc=1, device_id=device, device_id_type=MESH)

    def half_of(ref, which, first, size):
        return ref[:, pl.ds(pl.multiple_of(first + which * size, 128), size)]

    for i, ref in enumerate((wk_ref, wv_ref, wq_ref)):
        cols = slice(i * part_q, (i + 1) * part_q)
        w_qkv[own(0), cols] = half_of(ref, core, 0, part_q)
        g_qkv[:, cols] = half_of(ref, other, 0, part_q)
    w_out[own(1), :] = half_of(wo_ref, core, 0, part_d)
    g_out[...] = half_of(wo_ref, other, 0, part_d)
    for i in range(2):
        cols = slice(i * part_g, (i + 1) * part_g)
        w_glu[own(2), cols] = half_of(wg_ref, core, 2 * i * part_g, part_g)
        g_glu[:, cols] = half_of(wg_ref, other, 2 * i * part_g, part_g)
    w_proj[own(3), :] = half_of(wp_ref, core, 0, part_d)
    g_proj[...] = half_of(wp_ref, other, 0, part_d)
    res[core] = half_of(frames_ref, core, 0, part_d)
    g_frames[...] = half_of(frames_ref, other, 0, part_d)
    pl.semaphore_wait(barrier, 6)
    for w in range(4):
        give(w).start()
    swap_res = copy(g_frames, res.at[core], e_send.at[0], e_recv.at[0], pair)
    advance()

    mine = 2 + core
    norm_rows(frames_ref, gain_a_ref, norm.at[mine])
    meta[mine, 0:1, :] = jnp.full((1, 128), count_ref[0], jnp.int32)
    for b in range(4):
        meta[mine, 1 + b : 2 + b, :] = jnp.full((1, 128), look_ref[0, b], jnp.int32)
    norm_pair = copy(norm.at[mine], norm.at[mine], n_send.at[0], n_recv.at[0], pair)
    norm_next = copy(norm.at[mine], norm.at[core], n_send.at[1], n_recv.at[1], here(t + 2))
    norm_relay = copy(norm.at[core], norm.at[core], n_send.at[2], n_recv.at[2], pair)
    meta_pair = copy(meta.at[mine], meta.at[mine], m_send.at[0], m_recv.at[0], pair)
    meta_next = copy(meta.at[mine], meta.at[core], m_send.at[1], m_recv.at[1], here(t + 2))
    meta_relay = copy(meta.at[core], meta.at[core], m_send.at[2], m_recv.at[2], pair)

    @pl.when(t + 2 < n)
    def _():
        norm_next.start()
        meta_next.start()

    norm_pair.start()
    meta_pair.start()
    swap_res.start()

    @pl.when(t < 2)
    def _():
        for i in range(2):
            norm[i] = jnp.zeros(norm.shape[1:], BF16)
            meta[i] = jnp.zeros(meta.shape[1:], jnp.int32)

    advance()
    advance()

    @pl.when(t >= 2)
    def _():
        norm_next.wait_recv()
        meta_next.wait_recv()
        norm_relay.start()
        meta_relay.start()

    norm_pair.wait_recv()
    meta_pair.wait_recv()
    swap_res.wait_recv()
    advance()

    @pl.when(t >= 2)
    def _():
        norm_relay.wait_recv()
        meta_relay.wait_recv()

    ready(0)

    @pl.loop(0, 2 * part_q // TILE)
    def _(j):
        cols = pl.ds(pl.multiple_of(j * TILE, TILE), TILE)
        for i in range(4):
            kv_s[i * length : (i + 1) * length, cols] = jnp.dot(
                norm[i], w_qkv[:, cols], preferred_element_type=F32
            ).astype(BF16)

    ready(1)
    for i in range(2):
        q_s[i * length : (i + 1) * length, :] = jnp.dot(
            norm[2 + i], w_qkv[:, 2 * part_q :], preferred_element_type=F32
        ).astype(BF16)
    advance()

    lane = lax.broadcasted_iota(jnp.int32, (1, 128), 1)

    def hidden(span):
        hide = []
        for b in range(3 * length // 128):
            limit = meta[span + b * 128 // length][0:1, :] - b * 128 % length
            seen = lane < limit
            if b * 128 < 2 * length:
                allowed = 1 + b * 128 // (length // 2)
                seen = seen & (meta[2 + span][allowed : allowed + 1, :] > 0)
            hide.append(jnp.where(seen, 0.0, -1e30))
        return jnp.concatenate(hide, axis=1)

    factor = math.log2(math.e) / math.sqrt(HEAD_DIM)

    def attend_head(span, head, hide):
        first = head * HEAD_DIM
        lo = first // 128 * 128
        hi = -(-(first + HEAD_DIM) // 128) * 128
        inside = lax.broadcasted_iota(jnp.int32, (length, hi - lo), 1) + lo
        inside = (inside >= first) & (inside < first + HEAD_DIM)
        q_at = slice(span * length, (span + 1) * length)
        k_at = slice(span * length, (span + 3) * length)
        q_head = jnp.where(inside, q_s[q_at, lo:hi].astype(F32), 0.0).astype(BF16)
        scores = lax.dot_general(
            q_head, kv_s[k_at, lo:hi], (((1,), (1,)), ((), ())), preferred_element_type=F32
        )
        scores = scores * factor + hide
        top = jnp.max(scores, axis=1, keepdims=True)
        expo = jnp.exp2(scores - top)
        total = jnp.sum(expo, axis=1, keepdims=True)
        context = jnp.dot(
            expo.astype(BF16), kv_s[k_at, part_q + lo : part_q + hi], preferred_element_type=F32
        )
        context = context / total
        before = ctx_s[core, q_at, lo:hi].astype(F32)
        ctx_s[core, q_at, lo:hi] = jnp.where(inside, context, before).astype(BF16)

    ctx_s[core] = jnp.zeros(ctx_s.shape[1:], BF16)
    for span in range(2):
        hide = hidden(span)
        for head in range(HEADS // 2):
            attend_head(span, head, hide)
            if head == 1:
                advance()

    swap_ctx = copy(ctx_s.at[core], ctx_s.at[core], e_send.at[1], e_recv.at[1], pair)
    swap_ctx.start()
    ready(2)
    swap_ctx.wait_recv()

    @pl.loop(0, part_d // TILE)
    def _(j):
        cols = pl.ds(pl.multiple_of(j * TILE, TILE), TILE)
        add = jnp.dot(ctx_s[0], w_out[:part_q, cols], preferred_element_type=F32)
        add = add + jnp.dot(ctx_s[1], w_out[part_q:, cols], preferred_element_type=F32)
        for i in range(2):
            at = slice(i * length, (i + 1) * length)
            mid_s[core, at, cols] = (res[i, :, cols].astype(F32) + add[at]).astype(BF16)

    swap_mid = copy(mid_s.at[core], mid_s.at[core], e_send.at[2], e_recv.at[2], pair)
    swap_mid.start()
    advance()
    swap_mid.wait_recv()

    @pl.loop(0, 2 * length // 32)
    def _(j):
        at = pl.ds(pl.multiple_of(j * 32, 32), 32)
        xf = jnp.concatenate([mid_s[0, at, :], mid_s[1, at, :]], axis=1).astype(F32)
        mean = jnp.mean(xf, axis=-1, keepdims=True)
        centered = xf - mean
        var = jnp.mean(centered * centered, axis=-1, keepdims=True)
        gain = gain_c_ref[...].reshape(1, -1)
        normc_s[at, :] = (centered * lax.rsqrt(var + 1e-05) * gain).astype(BF16)

    ready(3, 4)

    @pl.loop(0, part_g // TILE)
    def _(j):
        cols = pl.ds(pl.multiple_of(j * TILE, TILE), TILE)
        gate_cols = pl.ds(pl.multiple_of(part_g + j * TILE, TILE), TILE)
        for i in range(2):
            at = slice(i * length, (i + 1) * length)
            left = jnp.dot(normc_s[at, :], w_glu[:, cols], preferred_element_type=F32)
            right = jnp.dot(normc_s[at, :], w_glu[:, gate_cols], preferred_element_type=F32)
            live = lax.broadcasted_iota(jnp.int32, (length, 1), 0) < meta[2 + i][0:1, 0:1]
            gated = jnp.where(live, left * jax.nn.sigmoid(right), 0.0).astype(BF16)
            gpad[16 + i * length : 16 + (i + 1) * length, cols] = gated.astype(F32)
            if i == 0:
                hsend[0, :, cols] = gated[0:16]
            else:
                hsend[1, :, cols] = gated[length - 16 : length]

    below = copy(hsend.at[1], hrecv.at[0], h_send.at[0], h_recv.at[0], here(t + 2))
    above = copy(hsend.at[0], hrecv.at[1], h_send.at[1], h_recv.at[1], here(t - 2))

    @pl.when(t + 2 < n)
    def _():
        below.start()

    @pl.when(t >= 2)
    def _():
        above.start()

    while (5, hops_a - 1) not in stepped:
        advance()

    @pl.when(t >= 2)
    def _():
        below.wait_recv()
        gpad[0:16, :] = hrecv[0].astype(F32)

    @pl.when(t < 2)
    def _():
        gpad[0:16, :] = jnp.zeros((16, part_g), F32)

    @pl.when(t + 2 < n)
    def _():
        above.wait_recv()
        gpad[16 + 2 * length : 32 + 2 * length, :] = hrecv[1].astype(F32)

    @pl.when(t + 2 >= n)
    def _():
        gpad[16 + 2 * length : 32 + 2 * length, :] = jnp.zeros((16, part_g), F32)

    strip = 128

    @pl.loop(0, part_g // 128)
    def _(j):
        cols = pl.ds(pl.multiple_of(j * 128, 128), 128)
        wide = pl.ds(pl.multiple_of(core * part_g + j * 128, 128), 128)
        for start in range(0, 2 * length, strip):
            conv = jnp.zeros((strip, 128), F32)
            for shift in range(8):
                moved = gpad[start + shift : start + shift + strip + 24, cols]
                for at in range(shift, 32, 8):
                    if at >= 1:
                        conv = conv + taps_ref[at - 1 : at, wide] * moved[at - shift : at - shift + strip]
            pre = conv * scale_ref[:, wide] + shift_ref[:, wide]
            act_s[core, start : start + strip, cols] = (pre * jax.nn.sigmoid(pre)).astype(BF16)

    swap_act = copy(act_s.at[core], act_s.at[core], e_send.at[3], e_recv.at[3], pair)
    swap_act.start()
    ready(5)
    swap_act.wait_recv()

    def result(span, cols):
        at = pl.ds(pl.multiple_of(span * length, length), length)
        add = jnp.dot(act_s[0, at, :], w_proj[:part_g, cols], preferred_element_type=F32)
        add = add + jnp.dot(act_s[1, at, :], w_proj[part_g:, cols], preferred_element_type=F32)
        return (mid_s[core, at, cols].astype(F32) + add).astype(BF16)

    @pl.loop(0, part_d // TILE)
    def _(j):
        cols = pl.ds(pl.multiple_of(j * TILE, TILE), TILE)
        osend[:, cols] = result(other, cols)

    swap_out = copy(osend, orecv, e_send.at[4], e_recv.at[4], pair)
    swap_out.start()

    @pl.loop(0, part_d // TILE)
    def _(j):
        cols = pl.ds(pl.multiple_of(j * TILE, TILE), TILE)
        wide = pl.ds(pl.multiple_of(core * part_d + j * TILE, TILE), TILE)
        out_ref[:, wide] = result(core, cols)

    swap_out.wait_recv()
    out_ref[:, pl.ds(pl.multiple_of(other * part_d, 128), part_d)] = orecv[...]

    for p in range(len(pieces)):
        for side, hops in sides:
            for hop in range(hops):
                ring(p, side, hop).wait_send()
                over_x(p, side, hop).wait_send()
    for w in range(4):
        give(w).wait_send()
    for swap in (swap_res, swap_ctx, swap_mid, swap_act, swap_out, norm_pair, meta_pair):
        swap.wait_send()

    @pl.when(t + 2 < n)
    def _():
        norm_next.wait_send()
        meta_next.wait_send()
        below.wait_send()

    @pl.when(t >= 2)
    def _():
        norm_relay.wait_send()
        meta_relay.wait_send()
        above.wait_send()


def fused(
    n, frames, frame_count, lookback_mask, attn_gain, w_query, w_key, w_value, w_out, conv_gain,
    w_glu, depthwise, conv_scale, conv_shift, w_proj,
):
    length, model = frames.shape
    width = w_query.shape[1]
    half = w_glu.shape[1] // 2
    chips = n // 2
    inside, scalars = (pl.BlockSpec(memory_space=m) for m in (pltpu.VMEM, pltpu.SMEM))
    dma = pltpu.SemaphoreType.DMA
    params = 3 * width * model + model * width + 2 * half * model + half * model
    return pl.pallas_call(
        functools.partial(block, n),
        out_shape=jax.ShapeDtypeStruct((length, model), BF16),
        in_specs=[inside, scalars, scalars] + [inside] * 11,
        out_specs=pl.BlockSpec(memory_space=pltpu.VMEM),
        scratch_shapes=[
            pltpu.VMEM((model, 3 * width // 2), BF16),
            pltpu.VMEM((width, model // 2), BF16),
            pltpu.VMEM((model, half), BF16),
            pltpu.VMEM((half, model // 2), BF16),
            pltpu.VMEM((model // n, 3 * width // 2), BF16),
            pltpu.VMEM((width // n, model // 2), BF16),
            pltpu.VMEM((model // n, half), BF16),
            pltpu.VMEM((half // n, model // 2), BF16),
            pltpu.VMEM((length, model // 2), BF16),
            pltpu.VMEM((2, length, model // 2), BF16),
            pltpu.VMEM((4, length, model), BF16),
            pltpu.VMEM((4, 8, 128), jnp.int32),
            pltpu.VMEM((2 * length, width // 2), BF16),
            pltpu.VMEM((4 * length, width), BF16),
            pltpu.VMEM((2, 2 * length, width // 2), BF16),
            pltpu.VMEM((2, 2 * length, model // 2), BF16),
            pltpu.VMEM((2 * length, model), BF16),
            pltpu.VMEM((2 * length + 32, half // 2), F32),
            pltpu.VMEM((2, 2 * length, half // 2), BF16),
            pltpu.VMEM((2, 16, half // 2), BF16),
            pltpu.VMEM((2, 16, half // 2), BF16),
            pltpu.VMEM((length, model // 2), BF16),
            pltpu.VMEM((length, model // 2), BF16),
            dma((6, chips - 1)), dma((6, chips - 1)),
            dma((6, chips - 1)), dma((6, chips - 1)),
            dma((4,)), dma((4,)), dma((3,)), dma((3,)), dma((3,)), dma((3,)),
            dma((2,)), dma((2,)), dma((5,)), dma((5,)),
        ],
        compiler_params=pltpu.CompilerParams(
            collective_id=0, has_side_effects=True, vmem_limit_bytes=56 * 1024 * 1024
        ),
        cost_estimate=pl.CostEstimate(
            flops=2 * length * params, bytes_accessed=2 * params, transcendentals=length * half
        ),
    )(
        frames, frame_count, lookback_mask, attn_gain, w_query, w_key, w_value, w_out,
        conv_gain, w_glu, depthwise, conv_scale.reshape(1, -1),
        conv_shift.reshape(1, -1), w_proj,
    )


def shards(groups, *args):
    n = lax.axis_size("tm")
    frames, w_query, w_out, w_glu, w_proj = args[0], args[4], args[7], args[9], args[13]
    whole = all(w.shape[0] % 16 == 0 and w.shape[0] >= 48 for w in (w_query, w_out, w_glu, w_proj))
    tiles = all(
        w.shape[1] % TILE == 0 for w in (w_query, w_out, w_proj)
    ) and w_glu.shape[1] % (4 * TILE) == 0
    if groups == 2 and n % 8 == 0 and whole and tiles and frames.shape[0] % 256 == 0:
        return fused(n, *args)
    return plain(*args)


def solution(mesh):
    return jax.shard_map(
        functools.partial(shards, mesh.shape["groups"]),
        mesh=mesh,
        in_specs=(
            P(("groups", "tm"), None),
            P(("groups", "tm")),
            P(("groups", "tm"), None),
            P(),
            P("tm", None),
            P("tm", None),
            P("tm", None),
            P("tm", None),
            P(),
            P("tm", None),
            P(),
            P(),
            P(),
            P("tm", None),
        ),
        out_specs=P(("groups", "tm"), None),
        check_vma=False,
    )
```

```python
import functools
import math

import jax
import jax.numpy as jnp
from jax import lax
from jax.experimental import pallas as pl
from jax.experimental.pallas import tpu as pltpu
from jax.sharding import PartitionSpec as P

HEADS = 8
HEAD_DIM = 96
KERNEL = 31


def shifted(block, axis, distance):
    devices = range(lax.axis_size(axis))
    route = [(i - distance, i) for i in devices if i - distance in devices]
    return lax.ppermute(block, axis, route)


def with_halo(value, sides, width):
    for axis, dim in sides:
        size, length = (lax.axis_size(axis), value.shape[dim])
        up = [(i, (i + 1) % size) for i in range(size - 1)]
        down = [(j, i) for i, j in up]
        last = lax.slice_in_dim(value, length - width, length, axis=dim)
        first = lax.slice_in_dim(value, 0, width, axis=dim)
        before = lax.ppermute(last, axis, up)
        after = lax.ppermute(first, axis, down)
        value = jnp.concatenate([before, value, after], axis=dim)
    return value


def normalize(x, gain):
    xf = x.astype(jnp.float32)
    mean = jnp.mean(xf, axis=-1, keepdims=True)
    centered = xf - mean
    var = jnp.mean(centered * centered, axis=-1, keepdims=True)
    return (centered * lax.rsqrt(var + 1e-05) * gain).astype(jnp.bfloat16)


def add_rows(left, piece):
    return jnp.dot(left, piece, preferred_element_type=jnp.float32)


def attend(query_c, keys, values, counts, allowed):
    width = query_c.shape[0]
    pos = jnp.arange(3 * width, dtype=jnp.int32)
    section = pos // width
    place = pos % width
    limit = jnp.where(section == 0, counts[0], jnp.where(section == 1, counts[1], counts[2]))
    block = pos // (width // 2)
    allow = jnp.sum(
        (block[:, None] == jnp.arange(4, dtype=jnp.int32)[None, :]) * allowed[None, :], axis=1
    ) + (block >= 4)
    visible = (place < limit) & (allow > 0)
    factor = 1.0 / math.sqrt(HEAD_DIM)

    def one_head(head):
        start = head * HEAD_DIM
        q_head = lax.dynamic_slice_in_dim(query_c, start, HEAD_DIM, 1)
        k_head = lax.dynamic_slice_in_dim(keys, start, HEAD_DIM, 1)
        v_head = lax.dynamic_slice_in_dim(values, start, HEAD_DIM, 1)
        scores = (
            lax.dot_general(
                q_head, k_head, (((1,), (1,)), ((), ())), preferred_element_type=jnp.float32
            )
            * factor
        )
        scores = jnp.where(visible[None, :], scores, -jnp.inf)
        top = jnp.max(scores, axis=1, keepdims=True)
        expo = jnp.exp(scores - top)
        weights = (expo / jnp.sum(expo, axis=1, keepdims=True)).astype(jnp.bfloat16)
        return jnp.dot(weights, v_head, preferred_element_type=jnp.float32).astype(jnp.bfloat16)

    stacked = lax.map(one_head, jnp.arange(HEADS, dtype=jnp.int32))
    return jnp.transpose(stacked, (1, 0, 2)).reshape(width, HEADS * HEAD_DIM)


def plain(
    frames,
    frame_count,
    lookback_mask,
    attn_gain,
    w_query,
    w_key,
    w_value,
    w_out,
    conv_gain,
    w_glu,
    depthwise,
    conv_scale,
    conv_shift,
    w_proj,
):
    width = frames.shape[0]
    conv_width = w_proj.shape[0] * lax.axis_size("tm")
    norm_a = normalize(frames, attn_gain)
    query = add_rows(norm_a, lax.all_gather(w_query, "tm", axis=0, tiled=True))
    key = add_rows(norm_a, lax.all_gather(w_key, "tm", axis=0, tiled=True))
    value = add_rows(norm_a, lax.all_gather(w_value, "tm", axis=0, tiled=True))
    query = query.astype(jnp.bfloat16)
    key = key.astype(jnp.bfloat16)
    value = value.astype(jnp.bfloat16)
    own = (key, value, frame_count)
    received = []
    current = own
    for step in range(2):
        current = shifted((current[0], current[1], current[2]), "tm", 1)
        received.append(current)
    nearer, farther = (received[0], received[1])
    keys = jnp.concatenate([farther[0], nearer[0], key], axis=0)
    values = jnp.concatenate([farther[1], nearer[1], value], axis=0)
    counts = jnp.concatenate([farther[2], nearer[2], frame_count])
    context = attend(query, keys, values, counts, lookback_mask[0])
    attn_sum = add_rows(context, lax.all_gather(w_out, "tm", axis=0, tiled=True))
    mid = (frames.astype(jnp.float32) + attn_sum).astype(jnp.bfloat16)
    norm_c = normalize(mid, conv_gain)
    glu_in = add_rows(norm_c, lax.all_gather(w_glu, "tm", axis=0, tiled=True))
    live = jnp.arange(width, dtype=jnp.int32) < frame_count[0]
    gated = jnp.where(
        live[:, None], glu_in[:, :conv_width] * jax.nn.sigmoid(glu_in[:, conv_width:]), 0.0
    ).astype(jnp.bfloat16)
    half = KERNEL // 2
    padded = with_halo(gated, (("tm", 0),), half)
    conv = jnp.zeros((width, conv_width), jnp.float32)
    for tap in range(KERNEL):
        conv = conv + depthwise[tap] * padded[tap : tap + width].astype(jnp.float32)
    activated = jax.nn.silu(conv * conv_scale + conv_shift).astype(jnp.bfloat16)
    conv_sum = add_rows(activated, lax.all_gather(w_proj, "tm", axis=0, tiled=True))
    return (mid.astype(jnp.float32) + conv_sum).astype(jnp.bfloat16)


F32 = jnp.float32
BF16 = jnp.bfloat16
MESH = pl.DeviceIdType.MESH
TILE = 256


def norm_rows(source, gain_ref, target):
    rows = source.shape[0]

    @pl.loop(0, rows // 32)
    def _(step):
        at = pl.ds(pl.multiple_of(step * 32, 32), 32)
        xf = source[at, :].astype(F32)
        mean = jnp.mean(xf, axis=-1, keepdims=True)
        centered = xf - mean
        var = jnp.mean(centered * centered, axis=-1, keepdims=True)
        target[at, :] = (centered * lax.rsqrt(var + 1e-05) * gain_ref[...].reshape(1, -1)).astype(BF16)


def block(
    n,
    frames_ref, count_ref, look_ref, gain_a_ref, wq_ref, wk_ref, wv_ref, wo_ref, gain_c_ref,
    wg_ref, taps_ref, scale_ref, shift_ref, wp_ref,
    out_ref,
    w_qkv, w_out, w_glu, w_proj, g_qkv, g_out, g_glu, g_proj, g_frames, res, norm, meta,
    q_s, kv_s, ctx_s, mid_s, normc_s, gpad, act_s, hsend, hrecv, osend, orecv,
    ring_send, ring_recv, x_send, x_recv, c_send, c_recv, n_send, n_recv, m_send, m_recv,
    h_send, h_recv, e_send, e_recv,
):
    g = lax.axis_index("groups")
    t = lax.axis_index("tm")
    core = lax.rem(t, 2)
    other = 1 - core
    chip = t // 2
    chips = n // 2
    deep = chips // 2
    hops_a, hops_b = chips // 2, chips // 2 - 1
    place = jnp.where(lax.rem(chip, 2) == 0, chip // 2, chips - 1 - chip // 2)
    turn = 1 - 2 * core

    def at_place(r):
        r = lax.rem(r + 2 * chips, chips)
        return jnp.where(r < deep, 2 * r, 2 * (chips - 1 - r) + 1)

    here = lambda index: (g, index)
    next_a = here(2 * at_place(place + turn) + core)
    next_b = here(2 * at_place(place - turn) + core)
    pair = here(t + turn)
    across = (1 - g, t)

    weights = (w_qkv, w_out, w_glu, w_proj)
    depth = tuple(w.shape[0] // n for w in weights)
    length, model = frames_ref.shape
    part_q, part_d, part_g = wq_ref.shape[1] // 2, model // 2, wg_ref.shape[1] // 4
    pieces = (
        (0, 0, 2 * part_q, 66),
        (0, 2 * part_q, part_q, 66),
        (1, 0, part_d, 66),
        (2, 0, part_g, 75),
        (2, part_g, part_g, 75),
        (3, 0, part_d, 66),
    )
    turns = (0, 0, 2, 3, 3, 4)

    def rows(p, owner, start, size):
        w, first = pieces[p][:2]
        at = pl.ds(pl.multiple_of(owner * 2 * depth[w], 16), 2 * depth[w])
        return weights[w].at[at, pl.ds(pl.multiple_of(first + start, 128), size)]

    def sizes(p):
        cols, share = pieces[p][2:]
        return cols, (share * cols + 6400) // 12800 * 128

    def copy(src, dst, send, recv, device):
        return pltpu.make_async_remote_copy(
            src_ref=src, dst_ref=dst, send_sem=send, recv_sem=recv,
            device_id=device, device_id_type=MESH,
        )

    def ring(p, side, hop):
        sign = turn if side == 0 else -turn
        cols, ringed = sizes(p)
        view = rows(p, at_place(place - sign * hop), g * (cols - ringed), ringed)
        slot = hop + side * hops_a
        target = next_a if side == 0 else next_b
        return copy(view, view, ring_send.at[p, slot], ring_recv.at[p, slot], target)

    def over_x(p, side, hop):
        owner = at_place(place - (turn if side == 0 else -turn) * (hop + 1))
        cols, ringed = sizes(p)
        view = rows(p, owner, g * ringed, cols - ringed)
        slot = hop + side * hops_a
        return copy(view, view, x_send.at[p, slot], x_recv.at[p, slot], across)

    sides = ((0, hops_a), (1, hops_b))
    own = lambda w: pl.ds(pl.multiple_of(t * depth[w], 16), depth[w])
    given = (g_qkv, g_out, g_glu, g_proj)

    def give(w):
        return copy(given[w], weights[w].at[own(w), :], c_send.at[w], c_recv.at[w], pair)

    got, stepped, rounds = set(), set(), []

    def begin(p):
        w = pieces[p][0]
        if w not in got:
            got.add(w)
            give(w).wait_recv()
        ring(p, 0, 0).start()
        ring(p, 1, 0).start()

    def step(p, hop):
        stepped.add((p, hop))
        for side, hops in sides:
            if hop < hops:
                ring(p, side, hop).wait_recv()
                if hop + 1 < hops:
                    ring(p, side, hop + 1).start()
                over_x(p, side, hop).start()

    def advance():
        number = len(rounds)
        rounds.append(number)
        for p, first in enumerate(turns):
            hop = number - first - 1
            if hop == -1:
                begin(p)
            if 0 <= hop < hops_a:
                step(p, hop)

    def ready(*which):
        for p in which:
            while (p, hops_a - 1) not in stepped:
                advance()
        for p in which:
            for side, hops in sides:
                for hop in range(hops):
                    over_x(p, side, hop).wait_recv()

    barrier = pltpu.get_barrier_semaphore()
    around = [here(lax.rem(t + n + d, n)) for d in (2, -2)]
    for device in [next_a, next_b, pair, across] + around:
        pl.semaphore_signal(barrier, inc=1, device_id=device, device_id_type=MESH)

    def half_of(ref, which, first, size):
        return ref[:, pl.ds(pl.multiple_of(first + which * size, 128), size)]

    for i, ref in enumerate((wk_ref, wv_ref, wq_ref)):
        cols = slice(i * part_q, (i + 1) * part_q)
        w_qkv[own(0), cols] = half_of(ref, core, 0, part_q)
        g_qkv[:, cols] = half_of(ref, other, 0, part_q)
    w_out[own(1), :] = half_of(wo_ref, core, 0, part_d)
    g_out[...] = half_of(wo_ref, other, 0, part_d)
    for i in range(2):
        cols = slice(i * part_g, (i + 1) * part_g)
        w_glu[own(2), cols] = half_of(wg_ref, core, 2 * i * part_g, part_g)
        g_glu[:, cols] = half_of(wg_ref, other, 2 * i * part_g, part_g)
    w_proj[own(3), :] = half_of(wp_ref, core, 0, part_d)
    g_proj[...] = half_of(wp_ref, other, 0, part_d)
    res[core] = half_of(frames_ref, core, 0, part_d)
    g_frames[...] = half_of(frames_ref, other, 0, part_d)
    pl.semaphore_wait(barrier, 6)
    for w in range(4):
        give(w).start()
    swap_res = copy(g_frames, res.at[core], e_send.at[0], e_recv.at[0], pair)
    advance()

    mine = 2 + core
    norm_rows(frames_ref, gain_a_ref, norm.at[mine])
    meta[mine, 0:1, :] = jnp.full((1, 128), count_ref[0], jnp.int32)
    for b in range(4):
        meta[mine, 1 + b : 2 + b, :] = jnp.full((1, 128), look_ref[0, b], jnp.int32)
    norm_pair = copy(norm.at[mine], norm.at[mine], n_send.at[0], n_recv.at[0], pair)
    norm_next = copy(norm.at[mine], norm.at[core], n_send.at[1], n_recv.at[1], here(t + 2))
    norm_relay = copy(norm.at[core], norm.at[core], n_send.at[2], n_recv.at[2], pair)
    meta_pair = copy(meta.at[mine], meta.at[mine], m_send.at[0], m_recv.at[0], pair)
    meta_next = copy(meta.at[mine], meta.at[core], m_send.at[1], m_recv.at[1], here(t + 2))
    meta_relay = copy(meta.at[core], meta.at[core], m_send.at[2], m_recv.at[2], pair)

    @pl.when(t + 2 < n)
    def _():
        norm_next.start()
        meta_next.start()

    norm_pair.start()
    meta_pair.start()
    swap_res.start()

    @pl.when(t < 2)
    def _():
        for i in range(2):
            norm[i] = jnp.zeros(norm.shape[1:], BF16)
            meta[i] = jnp.zeros(meta.shape[1:], jnp.int32)

    advance()
    advance()

    @pl.when(t >= 2)
    def _():
        norm_next.wait_recv()
        meta_next.wait_recv()
        norm_relay.start()
        meta_relay.start()

    norm_pair.wait_recv()
    meta_pair.wait_recv()
    swap_res.wait_recv()
    advance()

    @pl.when(t >= 2)
    def _():
        norm_relay.wait_recv()
        meta_relay.wait_recv()

    ready(0)

    @pl.loop(0, 2 * part_q // TILE)
    def _(j):
        cols = pl.ds(pl.multiple_of(j * TILE, TILE), TILE)
        for i in range(4):
            kv_s[i * length : (i + 1) * length, cols] = jnp.dot(
                norm[i], w_qkv[:, cols], preferred_element_type=F32
            ).astype(BF16)

    ready(1)
    for i in range(2):
        q_s[i * length : (i + 1) * length, :] = jnp.dot(
            norm[2 + i], w_qkv[:, 2 * part_q :], preferred_element_type=F32
        ).astype(BF16)
    advance()

    lane = lax.broadcasted_iota(jnp.int32, (1, 128), 1)

    def hidden(span):
        hide = []
        for b in range(3 * length // 128):
            limit = meta[span + b * 128 // length][0:1, :] - b * 128 % length
            seen = lane < limit
            if b * 128 < 2 * length:
                allowed = 1 + b * 128 // (length // 2)
                seen = seen & (meta[2 + span][allowed : allowed + 1, :] > 0)
            hide.append(jnp.where(seen, 0.0, -1e30))
        return jnp.concatenate(hide, axis=1)

    factor = math.log2(math.e) / math.sqrt(HEAD_DIM)

    def attend_head(span, head, hide):
        first = head * HEAD_DIM
        lo = first // 128 * 128
        hi = -(-(first + HEAD_DIM) // 128) * 128
        inside = lax.broadcasted_iota(jnp.int32, (length, hi - lo), 1) + lo
        inside = (inside >= first) & (inside < first + HEAD_DIM)
        q_at = slice(span * length, (span + 1) * length)
        k_at = slice(span * length, (span + 3) * length)
        q_head = jnp.where(inside, q_s[q_at, lo:hi].astype(F32), 0.0).astype(BF16)
        scores = lax.dot_general(
            q_head, kv_s[k_at, lo:hi], (((1,), (1,)), ((), ())), preferred_element_type=F32
        )
        scores = scores * factor + hide
        top = jnp.max(scores, axis=1, keepdims=True)
        expo = jnp.exp2(scores - top)
        total = jnp.sum(expo, axis=1, keepdims=True)
        context = jnp.dot(
            expo.astype(BF16), kv_s[k_at, part_q + lo : part_q + hi], preferred_element_type=F32
        )
        context = context / total
        before = ctx_s[core, q_at, lo:hi].astype(F32)
        ctx_s[core, q_at, lo:hi] = jnp.where(inside, context, before).astype(BF16)

    ctx_s[core] = jnp.zeros(ctx_s.shape[1:], BF16)
    for span in range(2):
        hide = hidden(span)
        for head in range(HEADS // 2):
            attend_head(span, head, hide)
            if head == 1:
                advance()

    swap_ctx = copy(ctx_s.at[core], ctx_s.at[core], e_send.at[1], e_recv.at[1], pair)
    swap_ctx.start()
    ready(2)
    swap_ctx.wait_recv()

    @pl.loop(0, part_d // TILE)
    def _(j):
        cols = pl.ds(pl.multiple_of(j * TILE, TILE), TILE)
        add = jnp.dot(ctx_s[0], w_out[:part_q, cols], preferred_element_type=F32)
        add = add + jnp.dot(ctx_s[1], w_out[part_q:, cols], preferred_element_type=F32)
        for i in range(2):
            at = slice(i * length, (i + 1) * length)
            mid_s[core, at, cols] = (res[i, :, cols].astype(F32) + add[at]).astype(BF16)

    swap_mid = copy(mid_s.at[core], mid_s.at[core], e_send.at[2], e_recv.at[2], pair)
    swap_mid.start()
    advance()
    swap_mid.wait_recv()

    @pl.loop(0, 2 * length // 32)
    def _(j):
        at = pl.ds(pl.multiple_of(j * 32, 32), 32)
        xf = jnp.concatenate([mid_s[0, at, :], mid_s[1, at, :]], axis=1).astype(F32)
        mean = jnp.mean(xf, axis=-1, keepdims=True)
        centered = xf - mean
        var = jnp.mean(centered * centered, axis=-1, keepdims=True)
        gain = gain_c_ref[...].reshape(1, -1)
        normc_s[at, :] = (centered * lax.rsqrt(var + 1e-05) * gain).astype(BF16)

    ready(3, 4)

    @pl.loop(0, part_g // TILE)
    def _(j):
        cols = pl.ds(pl.multiple_of(j * TILE, TILE), TILE)
        gate_cols = pl.ds(pl.multiple_of(part_g + j * TILE, TILE), TILE)
        for i in range(2):
            at = slice(i * length, (i + 1) * length)
            left = jnp.dot(normc_s[at, :], w_glu[:, cols], preferred_element_type=F32)
            right = jnp.dot(normc_s[at, :], w_glu[:, gate_cols], preferred_element_type=F32)
            live = lax.broadcasted_iota(jnp.int32, (length, 1), 0) < meta[2 + i][0:1, 0:1]
            gated = jnp.where(live, left * jax.nn.sigmoid(right), 0.0).astype(BF16)
            gpad[16 + i * length : 16 + (i + 1) * length, cols] = gated.astype(F32)
            if i == 0:
                hsend[0, :, cols] = gated[0:16]
            else:
                hsend[1, :, cols] = gated[length - 16 : length]

    below = copy(hsend.at[1], hrecv.at[0], h_send.at[0], h_recv.at[0], here(t + 2))
    above = copy(hsend.at[0], hrecv.at[1], h_send.at[1], h_recv.at[1], here(t - 2))

    @pl.when(t + 2 < n)
    def _():
        below.start()

    @pl.when(t >= 2)
    def _():
        above.start()

    while (5, hops_a - 1) not in stepped:
        advance()

    @pl.when(t >= 2)
    def _():
        below.wait_recv()
        gpad[0:16, :] = hrecv[0].astype(F32)

    @pl.when(t < 2)
    def _():
        gpad[0:16, :] = jnp.zeros((16, part_g), F32)

    @pl.when(t + 2 < n)
    def _():
        above.wait_recv()
        gpad[16 + 2 * length : 32 + 2 * length, :] = hrecv[1].astype(F32)

    @pl.when(t + 2 >= n)
    def _():
        gpad[16 + 2 * length : 32 + 2 * length, :] = jnp.zeros((16, part_g), F32)

    strip = 128

    @pl.loop(0, part_g // 128)
    def _(j):
        cols = pl.ds(pl.multiple_of(j * 128, 128), 128)
        wide = pl.ds(pl.multiple_of(core * part_g + j * 128, 128), 128)
        for start in range(0, 2 * length, strip):
            conv = jnp.zeros((strip, 128), F32)
            for shift in range(8):
                moved = gpad[start + shift : start + shift + strip + 24, cols]
                for at in range(shift, 32, 8):
                    if at >= 1:
                        conv = conv + taps_ref[at - 1 : at, wide] * moved[at - shift : at - shift + strip]
            pre = conv * scale_ref[:, wide] + shift_ref[:, wide]
            act_s[core, start : start + strip, cols] = (pre * jax.nn.sigmoid(pre)).astype(BF16)

    swap_act = copy(act_s.at[core], act_s.at[core], e_send.at[3], e_recv.at[3], pair)
    swap_act.start()
    ready(5)
    swap_act.wait_recv()

    def result(span, cols):
        at = pl.ds(pl.multiple_of(span * length, length), length)
        add = jnp.dot(act_s[0, at, :], w_proj[:part_g, cols], preferred_element_type=F32)
        add = add + jnp.dot(act_s[1, at, :], w_proj[part_g:, cols], preferred_element_type=F32)
        return (mid_s[core, at, cols].astype(F32) + add).astype(BF16)

    @pl.loop(0, part_d // TILE)
    def _(j):
        cols = pl.ds(pl.multiple_of(j * TILE, TILE), TILE)
        osend[:, cols] = result(other, cols)

    swap_out = copy(osend, orecv, e_send.at[4], e_recv.at[4], pair)
    swap_out.start()

    @pl.loop(0, part_d // TILE)
    def _(j):
        cols = pl.ds(pl.multiple_of(j * TILE, TILE), TILE)
        wide = pl.ds(pl.multiple_of(core * part_d + j * TILE, TILE), TILE)
        out_ref[:, wide] = result(core, cols)

    swap_out.wait_recv()
    out_ref[:, pl.ds(pl.multiple_of(other * part_d, 128), part_d)] = orecv[...]

    for p in range(len(pieces)):
        for side, hops in sides:
            for hop in range(hops):
                ring(p, side, hop).wait_send()
                over_x(p, side, hop).wait_send()
    for w in range(4):
        give(w).wait_send()
    for swap in (swap_res, swap_ctx, swap_mid, swap_act, swap_out, norm_pair, meta_pair):
        swap.wait_send()

    @pl.when(t + 2 < n)
    def _():
        norm_next.wait_send()
        meta_next.wait_send()
        below.wait_send()

    @pl.when(t >= 2)
    def _():
        norm_relay.wait_send()
        meta_relay.wait_send()
        above.wait_send()


def fused(
    n, frames, frame_count, lookback_mask, attn_gain, w_query, w_key, w_value, w_out, conv_gain,
    w_glu, depthwise, conv_scale, conv_shift, w_proj,
):
    length, model = frames.shape
    width = w_query.shape[1]
    half = w_glu.shape[1] // 2
    chips = n // 2
    inside, scalars = (pl.BlockSpec(memory_space=m) for m in (pltpu.VMEM, pltpu.SMEM))
    dma = pltpu.SemaphoreType.DMA
    params = 3 * width * model + model * width + 2 * half * model + half * model
    return pl.pallas_call(
        functools.partial(block, n),
        out_shape=jax.ShapeDtypeStruct((length, model), BF16),
        in_specs=[inside, scalars, scalars] + [inside] * 11,
        out_specs=pl.BlockSpec(memory_space=pltpu.VMEM),
        scratch_shapes=[
            pltpu.VMEM((model, 3 * width // 2), BF16),
            pltpu.VMEM((width, model // 2), BF16),
            pltpu.VMEM((model, half), BF16),
            pltpu.VMEM((half, model // 2), BF16),
            pltpu.VMEM((model // n, 3 * width // 2), BF16),
            pltpu.VMEM((width // n, model // 2), BF16),
            pltpu.VMEM((model // n, half), BF16),
            pltpu.VMEM((half // n, model // 2), BF16),
            pltpu.VMEM((length, model // 2), BF16),
            pltpu.VMEM((2, length, model // 2), BF16),
            pltpu.VMEM((4, length, model), BF16),
            pltpu.VMEM((4, 8, 128), jnp.int32),
            pltpu.VMEM((2 * length, width // 2), BF16),
            pltpu.VMEM((4 * length, width), BF16),
            pltpu.VMEM((2, 2 * length, width // 2), BF16),
            pltpu.VMEM((2, 2 * length, model // 2), BF16),
            pltpu.VMEM((2 * length, model), BF16),
            pltpu.VMEM((2 * length + 32, half // 2), F32),
            pltpu.VMEM((2, 2 * length, half // 2), BF16),
            pltpu.VMEM((2, 16, half // 2), BF16),
            pltpu.VMEM((2, 16, half // 2), BF16),
            pltpu.VMEM((length, model // 2), BF16),
            pltpu.VMEM((length, model // 2), BF16),
            dma((6, chips - 1)), dma((6, chips - 1)),
            dma((6, chips - 1)), dma((6, chips - 1)),
            dma((4,)), dma((4,)), dma((3,)), dma((3,)), dma((3,)), dma((3,)),
            dma((2,)), dma((2,)), dma((5,)), dma((5,)),
        ],
        compiler_params=pltpu.CompilerParams(
            collective_id=0, has_side_effects=True, vmem_limit_bytes=56 * 1024 * 1024
        ),
        cost_estimate=pl.CostEstimate(
            flops=2 * length * params, bytes_accessed=2 * params, transcendentals=length * half
        ),
    )(
        frames, frame_count, lookback_mask, attn_gain, w_query, w_key, w_value, w_out,
        conv_gain, w_glu, depthwise, conv_scale.reshape(1, -1),
        conv_shift.reshape(1, -1), w_proj,
    )


def shards(groups, *args):
    n = lax.axis_size("tm")
    frames, w_query, w_out, w_glu, w_proj = args[0], args[4], args[7], args[9], args[13]
    whole = all(w.shape[0] % 16 == 0 and w.shape[0] >= 48 for w in (w_query, w_out, w_glu, w_proj))
    tiles = all(
        w.shape[1] % TILE == 0 for w in (w_query, w_out, w_proj)
    ) and w_glu.shape[1] % (4 * TILE) == 0
    if groups == 2 and n % 8 == 0 and whole and tiles and frames.shape[0] % 256 == 0:
        return fused(n, *args)
    return plain(*args)


def solution(mesh):
    return jax.shard_map(
        functools.partial(shards, mesh.shape["groups"]),
        mesh=mesh,
        in_specs=(
            P(("groups", "tm"), None),
            P(("groups", "tm")),
            P(("groups", "tm"), None),
            P(),
            P("tm", None),
            P("tm", None),
            P("tm", None),
            P("tm", None),
            P(),
            P("tm", None),
            P(),
            P(),
            P(),
            P("tm", None),
        ),
        out_specs=P(("groups", "tm"), None),
        check_vma=False,
    )
```

```python
import functools
import math

import jax
import jax.numpy as jnp
from jax import lax
from jax.experimental import pallas as pl
from jax.experimental.pallas import tpu as pltpu
from jax.sharding import PartitionSpec as P

HEADS = 8
HEAD_DIM = 96
KERNEL = 31


def shifted(block, axis, distance):
    devices = range(lax.axis_size(axis))
    route = [(i - distance, i) for i in devices if i - distance in devices]
    return lax.ppermute(block, axis, route)


def with_halo(value, sides, width):
    for axis, dim in sides:
        size, length = (lax.axis_size(axis), value.shape[dim])
        up = [(i, (i + 1) % size) for i in range(size - 1)]
        down = [(j, i) for i, j in up]
        last = lax.slice_in_dim(value, length - width, length, axis=dim)
        first = lax.slice_in_dim(value, 0, width, axis=dim)
        before = lax.ppermute(last, axis, up)
        after = lax.ppermute(first, axis, down)
        value = jnp.concatenate([before, value, after], axis=dim)
    return value


def normalize(x, gain):
    xf = x.astype(jnp.float32)
    mean = jnp.mean(xf, axis=-1, keepdims=True)
    centered = xf - mean
    var = jnp.mean(centered * centered, axis=-1, keepdims=True)
    return (centered * lax.rsqrt(var + 1e-05) * gain).astype(jnp.bfloat16)


def add_rows(left, piece):
    return jnp.dot(left, piece, preferred_element_type=jnp.float32)


def attend(query_c, keys, values, counts, allowed):
    width = query_c.shape[0]
    pos = jnp.arange(3 * width, dtype=jnp.int32)
    section = pos // width
    place = pos % width
    limit = jnp.where(section == 0, counts[0], jnp.where(section == 1, counts[1], counts[2]))
    block = pos // (width // 2)
    allow = jnp.sum(
        (block[:, None] == jnp.arange(4, dtype=jnp.int32)[None, :]) * allowed[None, :], axis=1
    ) + (block >= 4)
    visible = (place < limit) & (allow > 0)
    factor = 1.0 / math.sqrt(HEAD_DIM)

    def one_head(head):
        start = head * HEAD_DIM
        q_head = lax.dynamic_slice_in_dim(query_c, start, HEAD_DIM, 1)
        k_head = lax.dynamic_slice_in_dim(keys, start, HEAD_DIM, 1)
        v_head = lax.dynamic_slice_in_dim(values, start, HEAD_DIM, 1)
        scores = (
            lax.dot_general(
                q_head, k_head, (((1,), (1,)), ((), ())), preferred_element_type=jnp.float32
            )
            * factor
        )
        scores = jnp.where(visible[None, :], scores, -jnp.inf)
        top = jnp.max(scores, axis=1, keepdims=True)
        expo = jnp.exp(scores - top)
        weights = (expo / jnp.sum(expo, axis=1, keepdims=True)).astype(jnp.bfloat16)
        return jnp.dot(weights, v_head, preferred_element_type=jnp.float32).astype(jnp.bfloat16)

    stacked = lax.map(one_head, jnp.arange(HEADS, dtype=jnp.int32))
    return jnp.transpose(stacked, (1, 0, 2)).reshape(width, HEADS * HEAD_DIM)


def plain(
    frames,
    frame_count,
    lookback_mask,
    attn_gain,
    w_query,
    w_key,
    w_value,
    w_out,
    conv_gain,
    w_glu,
    depthwise,
    conv_scale,
    conv_shift,
    w_proj,
):
    width = frames.shape[0]
    conv_width = w_proj.shape[0] * lax.axis_size("tm")
    norm_a = normalize(frames, attn_gain)
    query = add_rows(norm_a, lax.all_gather(w_query, "tm", axis=0, tiled=True))
    key = add_rows(norm_a, lax.all_gather(w_key, "tm", axis=0, tiled=True))
    value = add_rows(norm_a, lax.all_gather(w_value, "tm", axis=0, tiled=True))
    query = query.astype(jnp.bfloat16)
    key = key.astype(jnp.bfloat16)
    value = value.astype(jnp.bfloat16)
    own = (key, value, frame_count)
    received = []
    current = own
    for step in range(2):
        current = shifted((current[0], current[1], current[2]), "tm", 1)
        received.append(current)
    nearer, farther = (received[0], received[1])
    keys = jnp.concatenate([farther[0], nearer[0], key], axis=0)
    values = jnp.concatenate([farther[1], nearer[1], value], axis=0)
    counts = jnp.concatenate([farther[2], nearer[2], frame_count])
    context = attend(query, keys, values, counts, lookback_mask[0])
    attn_sum = add_rows(context, lax.all_gather(w_out, "tm", axis=0, tiled=True))
    mid = (frames.astype(jnp.float32) + attn_sum).astype(jnp.bfloat16)
    norm_c = normalize(mid, conv_gain)
    glu_in = add_rows(norm_c, lax.all_gather(w_glu, "tm", axis=0, tiled=True))
    live = jnp.arange(width, dtype=jnp.int32) < frame_count[0]
    gated = jnp.where(
        live[:, None], glu_in[:, :conv_width] * jax.nn.sigmoid(glu_in[:, conv_width:]), 0.0
    ).astype(jnp.bfloat16)
    half = KERNEL // 2
    padded = with_halo(gated, (("tm", 0),), half)
    conv = jnp.zeros((width, conv_width), jnp.float32)
    for tap in range(KERNEL):
        conv = conv + depthwise[tap] * padded[tap : tap + width].astype(jnp.float32)
    activated = jax.nn.silu(conv * conv_scale + conv_shift).astype(jnp.bfloat16)
    conv_sum = add_rows(activated, lax.all_gather(w_proj, "tm", axis=0, tiled=True))
    return (mid.astype(jnp.float32) + conv_sum).astype(jnp.bfloat16)


F32 = jnp.float32
BF16 = jnp.bfloat16
MESH = pl.DeviceIdType.MESH
TILE = 256


def norm_rows(source, gain_ref, target):
    rows = source.shape[0]

    @pl.loop(0, rows // 32)
    def _(step):
        at = pl.ds(pl.multiple_of(step * 32, 32), 32)
        xf = source[at, :].astype(F32)
        mean = jnp.mean(xf, axis=-1, keepdims=True)
        centered = xf - mean
        var = jnp.mean(centered * centered, axis=-1, keepdims=True)
        target[at, :] = (centered * lax.rsqrt(var + 1e-05) * gain_ref[...].reshape(1, -1)).astype(BF16)


def block(
    n,
    frames_ref, count_ref, look_ref, gain_a_ref, wq_ref, wk_ref, wv_ref, wo_ref, gain_c_ref,
    wg_ref, taps_ref, scale_ref, shift_ref, wp_ref,
    out_ref,
    w_qkv, w_out, w_glu, w_proj, g_qkv, g_out, g_glu, g_proj, g_frames, res, norm, meta,
    q_s, kv_s, ctx_s, mid_s, normc_s, gpad, act_s, hsend, hrecv, osend, orecv,
    ring_send, ring_recv, x_send, x_recv, c_send, c_recv, n_send, n_recv, m_send, m_recv,
    h_send, h_recv, e_send, e_recv,
):
    g = lax.axis_index("groups")
    t = lax.axis_index("tm")
    core = lax.rem(t, 2)
    other = 1 - core
    chip = t // 2
    chips = n // 2
    deep = chips // 2
    hops_a, hops_b = chips // 2, chips // 2 - 1
    place = jnp.where(lax.rem(chip, 2) == 0, chip // 2, chips - 1 - chip // 2)
    turn = 1 - 2 * core

    def at_place(r):
        r = lax.rem(r + 2 * chips, chips)
        return jnp.where(r < deep, 2 * r, 2 * (chips - 1 - r) + 1)

    here = lambda index: (g, index)
    next_a = here(2 * at_place(place + turn) + core)
    next_b = here(2 * at_place(place - turn) + core)
    pair = here(t + turn)
    across = (1 - g, t)

    weights = (w_qkv, w_out, w_glu, w_proj)
    depth = tuple(w.shape[0] // n for w in weights)
    length, model = frames_ref.shape
    part_q, part_d, part_g = wq_ref.shape[1] // 2, model // 2, wg_ref.shape[1] // 4
    pieces = (
        (0, 0, 2 * part_q, 50),
        (0, 2 * part_q, part_q, 66),
        (1, 0, part_d, 66),
        (2, 0, part_g, 50),
        (2, part_g, part_g, 75),
        (3, 0, part_d, 66),
    )
    turns = (0, 0, 1, 2, 2, 3)

    def rows(p, owner, start, size):
        w, first = pieces[p][:2]
        at = pl.ds(pl.multiple_of(owner * 2 * depth[w], 16), 2 * depth[w])
        return weights[w].at[at, pl.ds(pl.multiple_of(first + start, 128), size)]

    def sizes(p):
        cols, share = pieces[p][2:]
        return cols, (share * cols + 6400) // 12800 * 128

    def copy(src, dst, send, recv, device):
        return pltpu.make_async_remote_copy(
            src_ref=src, dst_ref=dst, send_sem=send, recv_sem=recv,
            device_id=device, device_id_type=MESH,
        )

    def ring(p, side, hop):
        sign = turn if side == 0 else -turn
        cols, ringed = sizes(p)
        view = rows(p, at_place(place - sign * hop), g * (cols - ringed), ringed)
        slot = hop + side * hops_a
        target = next_a if side == 0 else next_b
        return copy(view, view, ring_send.at[p, slot], ring_recv.at[p, slot], target)

    def over_x(p, side, hop):
        owner = at_place(place - (turn if side == 0 else -turn) * (hop + 1))
        cols, ringed = sizes(p)
        view = rows(p, owner, g * ringed, cols - ringed)
        slot = hop + side * hops_a
        return copy(view, view, x_send.at[p, slot], x_recv.at[p, slot], across)

    sides = ((0, hops_a), (1, hops_b))
    own = lambda w: pl.ds(pl.multiple_of(t * depth[w], 16), depth[w])
    given = (g_qkv, g_out, g_glu, g_proj)

    def give(w):
        return copy(given[w], weights[w].at[own(w), :], c_send.at[w], c_recv.at[w], pair)

    got, stepped, rounds = set(), set(), []

    def begin(p):
        w = pieces[p][0]
        if w not in got:
            got.add(w)
            give(w).wait_recv()
        ring(p, 0, 0).start()
        ring(p, 1, 0).start()

    def step(p, hop):
        stepped.add((p, hop))
        for side, hops in sides:
            if hop < hops:
                ring(p, side, hop).wait_recv()
                if hop + 1 < hops:
                    ring(p, side, hop + 1).start()
                over_x(p, side, hop).start()

    def advance():
        number = len(rounds)
        rounds.append(number)
        for p, first in enumerate(turns):
            hop = number - first - 1
            if hop == -1:
                begin(p)
            if 0 <= hop < hops_a:
                step(p, hop)

    def ready(*which):
        for p in which:
            while (p, hops_a - 1) not in stepped:
                advance()
        for p in which:
            for side, hops in sides:
                for hop in range(hops):
                    over_x(p, side, hop).wait_recv()

    barrier = pltpu.get_barrier_semaphore()
    around = [here(lax.rem(t + n + d, n)) for d in (2, -2)]
    for device in [next_a, next_b, pair, across] + around:
        pl.semaphore_signal(barrier, inc=1, device_id=device, device_id_type=MESH)

    def half_of(ref, which, first, size):
        return ref[:, pl.ds(pl.multiple_of(first + which * size, 128), size)]

    for i, ref in enumerate((wk_ref, wv_ref, wq_ref)):
        cols = slice(i * part_q, (i + 1) * part_q)
        w_qkv[own(0), cols] = half_of(ref, core, 0, part_q)
        g_qkv[:, cols] = half_of(ref, other, 0, part_q)
    w_out[own(1), :] = half_of(wo_ref, core, 0, part_d)
    g_out[...] = half_of(wo_ref, other, 0, part_d)
    for i in range(2):
        cols = slice(i * part_g, (i + 1) * part_g)
        w_glu[own(2), cols] = half_of(wg_ref, core, 2 * i * part_g, part_g)
        g_glu[:, cols] = half_of(wg_ref, other, 2 * i * part_g, part_g)
    w_proj[own(3), :] = half_of(wp_ref, core, 0, part_d)
    g_proj[...] = half_of(wp_ref, other, 0, part_d)
    res[core] = half_of(frames_ref, core, 0, part_d)
    g_frames[...] = half_of(frames_ref, other, 0, part_d)
    pl.semaphore_wait(barrier, 6)
    for w in range(4):
        give(w).start()
    swap_res = copy(g_frames, res.at[core], e_send.at[0], e_recv.at[0], pair)
    advance()

    mine = 2 + core
    norm_rows(frames_ref, gain_a_ref, norm.at[mine])
    meta[mine, 0:1, :] = jnp.full((1, 128), count_ref[0], jnp.int32)
    for b in range(4):
        meta[mine, 1 + b : 2 + b, :] = jnp.full((1, 128), look_ref[0, b], jnp.int32)
    norm_pair = copy(norm.at[mine], norm.at[mine], n_send.at[0], n_recv.at[0], pair)
    norm_next = copy(norm.at[mine], norm.at[core], n_send.at[1], n_recv.at[1], here(t + 2))
    norm_relay = copy(norm.at[core], norm.at[core], n_send.at[2], n_recv.at[2], pair)
    meta_pair = copy(meta.at[mine], meta.at[mine], m_send.at[0], m_recv.at[0], pair)
    meta_next = copy(meta.at[mine], meta.at[core], m_send.at[1], m_recv.at[1], here(t + 2))
    meta_relay = copy(meta.at[core], meta.at[core], m_send.at[2], m_recv.at[2], pair)

    @pl.when(t + 2 < n)
    def _():
        norm_next.start()
        meta_next.start()

    norm_pair.start()
    meta_pair.start()
    swap_res.start()

    @pl.when(t < 2)
    def _():
        for i in range(2):
            norm[i] = jnp.zeros(norm.shape[1:], BF16)
            meta[i] = jnp.zeros(meta.shape[1:], jnp.int32)

    advance()
    advance()

    @pl.when(t >= 2)
    def _():
        norm_next.wait_recv()
        meta_next.wait_recv()
        norm_relay.start()
        meta_relay.start()

    norm_pair.wait_recv()
    meta_pair.wait_recv()
    swap_res.wait_recv()
    advance()

    @pl.when(t >= 2)
    def _():
        norm_relay.wait_recv()
        meta_relay.wait_recv()

    ready(0)

    @pl.loop(0, 2 * part_q // TILE)
    def _(j):
        cols = pl.ds(pl.multiple_of(j * TILE, TILE), TILE)
        for i in range(4):
            kv_s[i * length : (i + 1) * length, cols] = jnp.dot(
                norm[i], w_qkv[:, cols], preferred_element_type=F32
            ).astype(BF16)

    ready(1)
    for i in range(2):
        q_s[i * length : (i + 1) * length, :] = jnp.dot(
            norm[2 + i], w_qkv[:, 2 * part_q :], preferred_element_type=F32
        ).astype(BF16)
    advance()

    lane = lax.broadcasted_iota(jnp.int32, (1, 128), 1)

    def hidden(span):
        hide = []
        for b in range(3 * length // 128):
            limit = meta[span + b * 128 // length][0:1, :] - b * 128 % length
            seen = lane < limit
            if b * 128 < 2 * length:
                allowed = 1 + b * 128 // (length // 2)
                seen = seen & (meta[2 + span][allowed : allowed + 1, :] > 0)
            hide.append(jnp.where(seen, 0.0, -1e30))
        return jnp.concatenate(hide, axis=1)

    factor = math.log2(math.e) / math.sqrt(HEAD_DIM)

    def attend_head(span, head, hide):
        first = head * HEAD_DIM
        lo = first // 128 * 128
        hi = -(-(first + HEAD_DIM) // 128) * 128
        inside = lax.broadcasted_iota(jnp.int32, (length, hi - lo), 1) + lo
        inside = (inside >= first) & (inside < first + HEAD_DIM)
        q_at = slice(span * length, (span + 1) * length)
        k_at = slice(span * length, (span + 3) * length)
        q_head = jnp.where(inside, q_s[q_at, lo:hi].astype(F32), 0.0).astype(BF16)
        scores = lax.dot_general(
            q_head, kv_s[k_at, lo:hi], (((1,), (1,)), ((), ())), preferred_element_type=F32
        )
        scores = scores * factor + hide
        top = jnp.max(scores, axis=1, keepdims=True)
        expo = jnp.exp2(scores - top)
        total = jnp.sum(expo, axis=1, keepdims=True)
        context = jnp.dot(
            expo.astype(BF16), kv_s[k_at, part_q + lo : part_q + hi], preferred_element_type=F32
        )
        context = context / total
        before = ctx_s[core, q_at, lo:hi].astype(F32)
        ctx_s[core, q_at, lo:hi] = jnp.where(inside, context, before).astype(BF16)

    ctx_s[core] = jnp.zeros(ctx_s.shape[1:], BF16)
    for span in range(2):
        hide = hidden(span)
        for head in range(HEADS // 2):
            attend_head(span, head, hide)
            if head == 1:
                advance()

    swap_ctx = copy(ctx_s.at[core], ctx_s.at[core], e_send.at[1], e_recv.at[1], pair)
    swap_ctx.start()
    ready(2)
    swap_ctx.wait_recv()

    @pl.loop(0, part_d // TILE)
    def _(j):
        cols = pl.ds(pl.multiple_of(j * TILE, TILE), TILE)
        add = jnp.dot(ctx_s[0], w_out[:part_q, cols], preferred_element_type=F32)
        add = add + jnp.dot(ctx_s[1], w_out[part_q:, cols], preferred_element_type=F32)
        for i in range(2):
            at = slice(i * length, (i + 1) * length)
            mid_s[core, at, cols] = (res[i, :, cols].astype(F32) + add[at]).astype(BF16)

    swap_mid = copy(mid_s.at[core], mid_s.at[core], e_send.at[2], e_recv.at[2], pair)
    swap_mid.start()
    advance()
    swap_mid.wait_recv()

    @pl.loop(0, 2 * length // 32)
    def _(j):
        at = pl.ds(pl.multiple_of(j * 32, 32), 32)
        xf = jnp.concatenate([mid_s[0, at, :], mid_s[1, at, :]], axis=1).astype(F32)
        mean = jnp.mean(xf, axis=-1, keepdims=True)
        centered = xf - mean
        var = jnp.mean(centered * centered, axis=-1, keepdims=True)
        gain = gain_c_ref[...].reshape(1, -1)
        normc_s[at, :] = (centered * lax.rsqrt(var + 1e-05) * gain).astype(BF16)

    ready(3, 4)

    @pl.loop(0, part_g // TILE)
    def _(j):
        cols = pl.ds(pl.multiple_of(j * TILE, TILE), TILE)
        gate_cols = pl.ds(pl.multiple_of(part_g + j * TILE, TILE), TILE)
        for i in range(2):
            at = slice(i * length, (i + 1) * length)
            left = jnp.dot(normc_s[at, :], w_glu[:, cols], preferred_element_type=F32)
            right = jnp.dot(normc_s[at, :], w_glu[:, gate_cols], preferred_element_type=F32)
            live = lax.broadcasted_iota(jnp.int32, (length, 1), 0) < meta[2 + i][0:1, 0:1]
            gated = jnp.where(live, left * jax.nn.sigmoid(right), 0.0).astype(BF16)
            gpad[16 + i * length : 16 + (i + 1) * length, cols] = gated.astype(F32)
            if i == 0:
                hsend[0, :, cols] = gated[0:16]
            else:
                hsend[1, :, cols] = gated[length - 16 : length]

    below = copy(hsend.at[1], hrecv.at[0], h_send.at[0], h_recv.at[0], here(t + 2))
    above = copy(hsend.at[0], hrecv.at[1], h_send.at[1], h_recv.at[1], here(t - 2))

    @pl.when(t + 2 < n)
    def _():
        below.start()

    @pl.when(t >= 2)
    def _():
        above.start()

    while (5, hops_a - 1) not in stepped:
        advance()

    @pl.when(t >= 2)
    def _():
        below.wait_recv()
        gpad[0:16, :] = hrecv[0].astype(F32)

    @pl.when(t < 2)
    def _():
        gpad[0:16, :] = jnp.zeros((16, part_g), F32)

    @pl.when(t + 2 < n)
    def _():
        above.wait_recv()
        gpad[16 + 2 * length : 32 + 2 * length, :] = hrecv[1].astype(F32)

    @pl.when(t + 2 >= n)
    def _():
        gpad[16 + 2 * length : 32 + 2 * length, :] = jnp.zeros((16, part_g), F32)

    strip = 128

    @pl.loop(0, part_g // 128)
    def _(j):
        cols = pl.ds(pl.multiple_of(j * 128, 128), 128)
        wide = pl.ds(pl.multiple_of(core * part_g + j * 128, 128), 128)
        for start in range(0, 2 * length, strip):
            conv = jnp.zeros((strip, 128), F32)
            for shift in range(8):
                moved = gpad[start + shift : start + shift + strip + 24, cols]
                for at in range(shift, 32, 8):
                    if at >= 1:
                        conv = conv + taps_ref[at - 1 : at, wide] * moved[at - shift : at - shift + strip]
            pre = conv * scale_ref[:, wide] + shift_ref[:, wide]
            act_s[core, start : start + strip, cols] = (pre * jax.nn.sigmoid(pre)).astype(BF16)

    swap_act = copy(act_s.at[core], act_s.at[core], e_send.at[3], e_recv.at[3], pair)
    swap_act.start()
    ready(5)
    swap_act.wait_recv()

    def result(span, cols):
        at = pl.ds(pl.multiple_of(span * length, length), length)
        add = jnp.dot(act_s[0, at, :], w_proj[:part_g, cols], preferred_element_type=F32)
        add = add + jnp.dot(act_s[1, at, :], w_proj[part_g:, cols], preferred_element_type=F32)
        return (mid_s[core, at, cols].astype(F32) + add).astype(BF16)

    @pl.loop(0, part_d // TILE)
    def _(j):
        cols = pl.ds(pl.multiple_of(j * TILE, TILE), TILE)
        osend[:, cols] = result(other, cols)

    swap_out = copy(osend, orecv, e_send.at[4], e_recv.at[4], pair)
    swap_out.start()

    @pl.loop(0, part_d // TILE)
    def _(j):
        cols = pl.ds(pl.multiple_of(j * TILE, TILE), TILE)
        wide = pl.ds(pl.multiple_of(core * part_d + j * TILE, TILE), TILE)
        out_ref[:, wide] = result(core, cols)

    swap_out.wait_recv()
    out_ref[:, pl.ds(pl.multiple_of(other * part_d, 128), part_d)] = orecv[...]

    for p in range(len(pieces)):
        for side, hops in sides:
            for hop in range(hops):
                ring(p, side, hop).wait_send()
                over_x(p, side, hop).wait_send()
    for w in range(4):
        give(w).wait_send()
    for swap in (swap_res, swap_ctx, swap_mid, swap_act, swap_out, norm_pair, meta_pair):
        swap.wait_send()

    @pl.when(t + 2 < n)
    def _():
        norm_next.wait_send()
        meta_next.wait_send()
        below.wait_send()

    @pl.when(t >= 2)
    def _():
        norm_relay.wait_send()
        meta_relay.wait_send()
        above.wait_send()


def fused(
    n, frames, frame_count, lookback_mask, attn_gain, w_query, w_key, w_value, w_out, conv_gain,
    w_glu, depthwise, conv_scale, conv_shift, w_proj,
):
    length, model = frames.shape
    width = w_query.shape[1]
    half = w_glu.shape[1] // 2
    chips = n // 2
    inside, scalars = (pl.BlockSpec(memory_space=m) for m in (pltpu.VMEM, pltpu.SMEM))
    dma = pltpu.SemaphoreType.DMA
    params = 3 * width * model + model * width + 2 * half * model + half * model
    return pl.pallas_call(
        functools.partial(block, n),
        out_shape=jax.ShapeDtypeStruct((length, model), BF16),
        in_specs=[inside, scalars, scalars] + [inside] * 11,
        out_specs=pl.BlockSpec(memory_space=pltpu.VMEM),
        scratch_shapes=[
            pltpu.VMEM((model, 3 * width // 2), BF16),
            pltpu.VMEM((width, model // 2), BF16),
            pltpu.VMEM((model, half), BF16),
            pltpu.VMEM((half, model // 2), BF16),
            pltpu.VMEM((model // n, 3 * width // 2), BF16),
            pltpu.VMEM((width // n, model // 2), BF16),
            pltpu.VMEM((model // n, half), BF16),
            pltpu.VMEM((half // n, model // 2), BF16),
            pltpu.VMEM((length, model // 2), BF16),
            pltpu.VMEM((2, length, model // 2), BF16),
            pltpu.VMEM((4, length, model), BF16),
            pltpu.VMEM((4, 8, 128), jnp.int32),
            pltpu.VMEM((2 * length, width // 2), BF16),
            pltpu.VMEM((4 * length, width), BF16),
            pltpu.VMEM((2, 2 * length, width // 2), BF16),
            pltpu.VMEM((2, 2 * length, model // 2), BF16),
            pltpu.VMEM((2 * length, model), BF16),
            pltpu.VMEM((2 * length + 32, half // 2), F32),
            pltpu.VMEM((2, 2 * length, half // 2), BF16),
            pltpu.VMEM((2, 16, half // 2), BF16),
            pltpu.VMEM((2, 16, half // 2), BF16),
            pltpu.VMEM((length, model // 2), BF16),
            pltpu.VMEM((length, model // 2), BF16),
            dma((6, chips - 1)), dma((6, chips - 1)),
            dma((6, chips - 1)), dma((6, chips - 1)),
            dma((4,)), dma((4,)), dma((3,)), dma((3,)), dma((3,)), dma((3,)),
            dma((2,)), dma((2,)), dma((5,)), dma((5,)),
        ],
        compiler_params=pltpu.CompilerParams(
            collective_id=0, has_side_effects=True, vmem_limit_bytes=56 * 1024 * 1024
        ),
        cost_estimate=pl.CostEstimate(
            flops=2 * length * params, bytes_accessed=2 * params, transcendentals=length * half
        ),
    )(
        frames, frame_count, lookback_mask, attn_gain, w_query, w_key, w_value, w_out,
        conv_gain, w_glu, depthwise, conv_scale.reshape(1, -1),
        conv_shift.reshape(1, -1), w_proj,
    )


def shards(groups, *args):
    n = lax.axis_size("tm")
    frames, w_query, w_out, w_glu, w_proj = args[0], args[4], args[7], args[9], args[13]
    whole = all(w.shape[0] % 16 == 0 and w.shape[0] >= 48 for w in (w_query, w_out, w_glu, w_proj))
    tiles = all(
        w.shape[1] % TILE == 0 for w in (w_query, w_out, w_proj)
    ) and w_glu.shape[1] % (4 * TILE) == 0
    if groups == 2 and n % 8 == 0 and whole and tiles and frames.shape[0] % 256 == 0:
        return fused(n, *args)
    return plain(*args)


def solution(mesh):
    return jax.shard_map(
        functools.partial(shards, mesh.shape["groups"]),
        mesh=mesh,
        in_specs=(
            P(("groups", "tm"), None),
            P(("groups", "tm")),
            P(("groups", "tm"), None),
            P(),
            P("tm", None),
            P("tm", None),
            P("tm", None),
            P("tm", None),
            P(),
            P("tm", None),
            P(),
            P(),
            P(),
            P("tm", None),
        ),
        out_specs=P(("groups", "tm"), None),
        check_vma=False,
    )
```
